128 devices in a mesh: ctx: 16 (over y_lo, z, core), head: 8 (over y_hi, x).
Axes of the slice: x: 4, y: 4 (y_hi: 2, y_lo: 2; y = y_hi * 2 + y_lo), z: 4, core: 2. Of those that a mesh axis runs over, the one named last changes fastest.
Arguments:
- queries: bfloat16 [64, 2, 8192], P('ctx', None, 'head'), may hold values from -16 to 16
- prefix_k: bfloat16 [262144, 1024], P('ctx', 'head'), may hold values from -10 to 10
- prefix_v: bfloat16 [262144, 1024], P('ctx', 'head'), may hold values from -7 to 7
- suffix_k: bfloat16 [96, 4096, 1024], P('ctx', None, 'head'), may hold values from -6 to 6
- suffix_v: bfloat16 [96, 4096, 1024], P('ctx', None, 'head'), may hold values from -6 to 6
- new_k: bfloat16 [64, 2, 1024], P('ctx', None, 'head'), may hold values from -10 to 10
- new_v: bfloat16 [64, 2, 1024], P('ctx', None, 'head'), may hold values from -6 to 6
- suffix_len: int32 [64], replicated, may hold values from 1 to 4096, 131072 in all
- owner_of: int32 [64], replicated, may hold values from 0 to 95, as said below
Outputs:
- attended: bfloat16 [64, 2, 8192], P('ctx')
The draws below stay inside these ranges and needn't reach their ends.
Inputs may be any that keep to these rules, and one draw needn't show every extreme that they name: `owner_of`: every request names a different slot; slot g belongs to ctx index g // 6; in every draw all 6 slots of some owner are taken.
All inputs are finite; a program needn't handle non-finite values.
Results may differ from the reference program's by a relative error of at most 0.0054.
Values may be sent and summed in bfloat16 or wider, within the bound.
No kernel may reach another device: no remote copies, remote signals or barrier semaphores. Data moves between devices by JAX's collectives and lax.ppermute only.
A program may use at most 64 MiB of HBM per device.

```python
import math
import jax
import jax.numpy as jnp
import numpy as np
from jax import lax

H = 64
KV = 8
HD = 128
NEWTOK = 2
KEYBLK = 2048
SUF = 4096
SLOTS = 6
PRE = 262144
R = 64
SLOTS_ALL = 96


def shared_directions(key):
    key = jax.random.fold_in(key, 101)
    return jnp.where(jax.random.bernoulli(key, 0.5, (KV, HD)), 1.0, -1.0).astype(jnp.float32)


def query_lean():
    return 1.8


def draw_queries(key, part):
    directions = shared_directions(key)
    key = jax.random.fold_in(key, 3)
    group_size = H // KV
    shape = (R, NEWTOK, KV, group_size, HD)
    noise = 2.4 * jax.random.truncated_normal(key, -4.0, 4.0, shape, jnp.float32)
    values_out = noise + query_lean() * directions[None, None, :, None, :]
    return values_out.reshape(R, NEWTOK, H * HD).astype(jnp.bfloat16)


def draw_prefix_k(key, part):
    key = jax.random.fold_in(key, 5)
    shape = (PRE, KV, HD)
    noise = jax.random.truncated_normal(key, -4.0, 4.0, shape, jnp.float32)
    return noise.reshape(PRE, KV * HD).astype(jnp.bfloat16)


def draw_prefix_v(key, part):
    key = jax.random.fold_in(key, 7)
    sign_key, cycle_key, phase_key, noise_key = jax.random.split(key, 4)
    columns = KV * HD
    offsets = jnp.where(jax.random.bernoulli(sign_key, 0.5, (columns,)), 1.0, -1.0).astype(jnp.float32)
    cycles = jax.random.randint(cycle_key, (columns,), 1, 4).astype(jnp.float32)
    phases = jax.random.uniform(phase_key, (columns,), jnp.float32, -math.pi, math.pi)
    along = jnp.arange(PRE, dtype=jnp.float32)[:, None] / PRE
    smooth = offsets[None, :] + 1.5 * jnp.sin(2.0 * math.pi * cycles[None, :] * along + phases[None, :])
    noise = jax.random.truncated_normal(noise_key, -4.0, 4.0, (PRE, columns), jnp.float32)
    return (smooth + noise).astype(jnp.bfloat16)


def draw_suffix_k(key, part):
    directions = shared_directions(key)
    key = jax.random.fold_in(key, 9)
    noise = jax.random.truncated_normal(key, -4.0, 4.0, (SLOTS_ALL, SUF, KV, HD), jnp.float32)
    lean = math.log(2.0 * PRE / SUF) / (query_lean() * math.sqrt(HD))
    values_out = noise + lean * directions[None, None]
    return values_out.reshape(SLOTS_ALL, SUF, KV * HD).astype(jnp.bfloat16)


def draw_new_k(key, part):
    directions = shared_directions(key)
    key = jax.random.fold_in(key, 13)
    noise = jax.random.truncated_normal(key, -4.0, 4.0, (R, NEWTOK, KV, HD), jnp.float32)
    lean = (math.log(PRE) + 2.0) / (query_lean() * math.sqrt(HD))
    values_out = noise + lean * directions[None, None]
    return values_out.reshape(R, NEWTOK, KV * HD).astype(jnp.bfloat16)


def draw_owner_of(key, part):
    key = jax.random.fold_in(key, 17)
    rank_key, full_key, order_key = jax.random.split(key, 3)
    ranks = jax.random.permutation(rank_key, SLOTS_ALL).astype(jnp.int32)
    slot_ids = jnp.arange(SLOTS_ALL, dtype=jnp.int32)
    full_owner = jax.random.randint(full_key, (), 0, SLOTS_ALL // SLOTS)
    boosted = 2 * (slot_ids // SLOTS == full_owner).astype(jnp.int32)
    boosted = boosted + ((slot_ids == 0) | (slot_ids == SLOTS_ALL - 1)).astype(jnp.int32)
    priority = ranks + SLOTS_ALL * boosted
    chosen = jnp.argsort(-priority)[:R].astype(jnp.int32)
    return chosen[jax.random.permutation(order_key, R)].astype(jnp.int32)


def shard_levels(rng, extent, cuts, low, largest):
    loudness, own = 1.0, jax.random.fold_in(rng, 6)
    for dim, blocks in cuts:
        heights = jnp.exp(jax.random.uniform(jax.random.fold_in(own, dim), (blocks,), jnp.float32, low / len(cuts), largest / len(cuts)))
        loudness = loudness * jnp.repeat(heights, extent[dim] // blocks).reshape([-1 if axis == dim else 1 for axis in range(len(extent))])
    return loudness


def profile(count, total, bound, skew):
    portions = [(1 << 20) // math.isqrt(standing ** skew) + 1 for standing in range(2, count + 1)]
    surplus, counts = total - bound - (count - 1), [1] * (count - 1)
    while surplus > 0:
        candidates = [i for i in range(count - 1) if counts[i] < bound]
        pool, remaining = sum([portions[i] for i in candidates]), surplus
        for i in candidates:
            more = min(bound - counts[i], max(1, remaining * portions[i] // pool), surplus)
            counts[i] = counts[i] + more
            surplus = surplus - more
    return np.array([bound] + counts)


def ragged_sizes(stream_key, count, total, reach, skew):
    if count == 2:
        one = jax.random.randint(stream_key, (), max(1, total - reach), min(reach, total - 1) + 1)
        return jnp.stack([one, total - one])
    tallies = jnp.asarray(profile(count, total, reach, skew), jnp.int32)
    couples = (count - 1) // 2
    source_of, sink = tallies[1:1 + 2 * couples:2], tallies[2:2 + 2 * couples:2]
    room = jnp.minimum(source_of - 1, reach - sink)
    passed = jax.random.randint(jax.random.fold_in(stream_key, 1), (couples,), 0, 1 << 20) % (room + 1)
    tallies = tallies.at[1:1 + 2 * couples:2].set(source_of - passed).at[2:2 + 2 * couples:2].set(sink + passed)
    return tallies[jax.random.permutation(jax.random.fold_in(stream_key, 2), count)]


def normal_values(stream_key, dims, spread, reach, shards=(), kind=jnp.bfloat16):
    values = spread * jax.random.normal(stream_key, dims, jnp.float32)
    if shards:
        values = values * shard_levels(stream_key, dims, shards, -0.22, 0.18)
    return jnp.clip(values, -reach, reach).astype(kind)


def setup_inputs(seed: int = 0) -> dict:
    arg_keys = jax.random.split(jax.random.key(seed), 10)
    return {
        "queries": draw_queries(jax.random.fold_in(arg_keys[9], 71), 0),
        "prefix_k": draw_prefix_k(jax.random.fold_in(arg_keys[9], 71), 0),
        "prefix_v": draw_prefix_v(jax.random.fold_in(arg_keys[9], 71), 0),
        "suffix_k": draw_suffix_k(jax.random.fold_in(arg_keys[9], 71), 0),
        "suffix_v": normal_values(arg_keys[4], (SLOTS_ALL, SUF, KV * HD), 1.0, 6.0, ((0, 16), (2, 8))),
        "new_k": draw_new_k(jax.random.fold_in(arg_keys[9], 71), 0),
        "new_v": normal_values(arg_keys[6], (R, NEWTOK, KV * HD), 1.0, 6.0, ((0, 16), (2, 8))),
        "suffix_len": ragged_sizes(arg_keys[7], R, R * SUF // 2, SUF, 2).astype(jnp.int32),
        "owner_of": draw_owner_of(jax.random.fold_in(arg_keys[9], 71), 0),
    }


NEG_BIG = -1e30


def merge_states(earlier, later):
    earlier_max, earlier_sum, earlier_mix = earlier
    later_max, later_sum, later_mix = later
    highest = jnp.maximum(earlier_max, later_max)
    earlier_scale = jnp.exp(earlier_max - highest)
    later_scale = jnp.exp(later_max - highest)
    return (highest, earlier_sum * earlier_scale + later_sum * later_scale,
            earlier_mix * earlier_scale[..., None] + later_mix * later_scale[..., None])


def empty_state(leading, head_dim):
    return (jnp.full(leading, NEG_BIG, jnp.float32), jnp.zeros(leading, jnp.float32),
            jnp.zeros(leading + (head_dim,), jnp.float32))


def suffix_block(query_heads, suffix_keys, suffix_values, lengths, fresh_keys, fresh_values):
    slot_count, step_count, heads_local, group_size, head_dim = query_heads.shape
    scaling = head_dim ** -0.5
    suffix_span = suffix_keys.shape[1]
    key_grid = suffix_keys.reshape(slot_count, suffix_span, heads_local, head_dim).astype(jnp.float32)
    value_grid = suffix_values.reshape(slot_count, suffix_span, heads_local, head_dim).astype(jnp.float32)
    fresh_key_grid = fresh_keys.reshape(slot_count, step_count, heads_local, head_dim).astype(jnp.float32)
    fresh_value_grid = fresh_values.reshape(slot_count, step_count, heads_local, head_dim).astype(jnp.float32)
    query_float = query_heads.astype(jnp.float32)
    scores = jnp.einsum("stgeh,skgh->stgek", query_float, key_grid) * scaling
    fresh_scores = jnp.einsum("stgeh,sugh->stgeu", query_float, fresh_key_grid) * scaling
    positions = lax.broadcasted_iota(jnp.int32, (slot_count, suffix_span), 1)
    live_keys = (positions < lengths[:, None])[:, None, None, None, :]
    token_rows = lax.broadcasted_iota(jnp.int32, (step_count, step_count), 0)
    token_cols = lax.broadcasted_iota(jnp.int32, (step_count, step_count), 1)
    causal = (token_cols <= token_rows)[None, :, None, None, :]
    highest = jnp.maximum(jnp.max(jnp.where(live_keys, scores, NEG_BIG), axis=-1),
                          jnp.max(jnp.where(causal, fresh_scores, NEG_BIG), axis=-1))
    weights = jnp.where(live_keys, jnp.exp(scores - highest[..., None]), 0.0).astype(jnp.bfloat16)
    fresh_weights = jnp.where(causal, jnp.exp(fresh_scores - highest[..., None]), 0.0).astype(jnp.bfloat16)
    weights_float = weights.astype(jnp.float32)
    fresh_float = fresh_weights.astype(jnp.float32)
    totals = jnp.sum(weights_float, axis=-1) + jnp.sum(fresh_float, axis=-1)
    mixture = jnp.einsum("stgek,skgh->stgeh", weights_float, value_grid)
    mixture = mixture + jnp.einsum("stgeu,sugh->stgeh", fresh_float, fresh_value_grid)
    return (highest, totals, mixture)


def reference(queries, prefix_k, prefix_v, suffix_k, suffix_v, new_k, new_v, suffix_len, owner_of):
    group_size = H // KV
    scaling = HD ** -0.5
    query_heads = queries.reshape(R, NEWTOK, KV, group_size, HD)
    query_float = query_heads.astype(jnp.float32)
    block_count = PRE // KEYBLK
    key_blocks = prefix_k.reshape(block_count, KEYBLK, KV, HD)
    value_blocks = prefix_v.reshape(block_count, KEYBLK, KV, HD)

    def visit(running, block_pair):
        key_block, value_block = block_pair
        scores = jnp.einsum("rtgeh,kgh->rtgek", query_float, key_block.astype(jnp.float32)) * scaling
        block_max = jnp.max(scores, axis=-1)
        weights = jnp.exp(scores - block_max[..., None]).astype(jnp.bfloat16).astype(jnp.float32)
        totals = jnp.sum(weights, axis=-1)
        mixture = jnp.einsum("rtgek,kgh->rtgeh", weights, value_block.astype(jnp.float32))
        return merge_states(running, (block_max, totals, mixture)), None

    prefix_state, unused = lax.scan(visit, empty_state((R, NEWTOK, KV, group_size), HD),
                                    (key_blocks, value_blocks))

    def one_request(request):
        slot = owner_of[request]
        return suffix_block(
            lax.dynamic_index_in_dim(query_heads, request, 0, keepdims=True),
            lax.dynamic_index_in_dim(suffix_k, slot, 0, keepdims=True),
            lax.dynamic_index_in_dim(suffix_v, slot, 0, keepdims=True),
            lax.dynamic_index_in_dim(suffix_len, request, 0, keepdims=True),
            lax.dynamic_index_in_dim(new_k, request, 0, keepdims=True),
            lax.dynamic_index_in_dim(new_v, request, 0, keepdims=True))

    suffix_states = lax.map(one_request, jnp.arange(R, dtype=jnp.int32))
    suffix_state = (suffix_states[0][:, 0], suffix_states[1][:, 0], suffix_states[2][:, 0])
    highest, totals, mixture = merge_states(prefix_state, suffix_state)
    attended = (mixture / totals[..., None]).astype(jnp.bfloat16)
    return attended.reshape(R, NEWTOK, H * HD)
```

```python
import functools

import jax
import jax.numpy as jnp
from jax import lax
from jax.experimental import pallas as pl
from jax.experimental.pallas import tpu as pltpu
from jax.sharding import PartitionSpec as P

H = 64
KV = 8
HD = 128
LOG2E = 1.4426950408889634
NEG_BIG = -1e30
SAFE_SUM = 2.0**60

CHUNK = 4096
TILE = 256

f32 = jnp.float32
bf16 = jnp.bfloat16


def dot(a, b):
    return lax.dot_general(a, b, (((1,), (0,)), ((), ())), preferred_element_type=f32)


def dot_t(a, b):
    return lax.dot_general(a, b, (((1,), (1,)), ((), ())), preferred_element_type=f32)


def lane_sum(x):
    return jnp.broadcast_to(jnp.sum(x, axis=1, keepdims=True), x.shape)


def pieces(x):
    first = x.astype(bf16)
    rest = x - first.astype(f32)
    second = rest.astype(bf16)
    third = (rest - second.astype(f32)).astype(bf16)
    return first, second, third


def spread_kernel(copies, q_ref, k_ref, v_ref, out_ref):
    rows = q_ref.shape[0] * q_ref.shape[1]
    width = q_ref.shape[2]
    block = jnp.concatenate(
        [
            q_ref[...].astype(f32).reshape(rows, width),
            k_ref[...].astype(f32).reshape(rows, HD),
            v_ref[...].astype(f32).reshape(rows, HD),
        ],
        axis=1,
    )
    out_ref[...] = jnp.concatenate([block] * copies, axis=0).astype(bf16)


def attend_kernel(
    scale, slots_ref, q_ref, pk_ref, pv_ref, sk_ref, sv_ref, out_ref,
    kbuf, vbuf, skbuf, svbuf, qrow, top, acc, total, qslot, oslot, lslot, ksem, vsem, ssem,
):
    req_rows = q_ref.shape[0]
    groups = (q_ref.shape[1] - 2 * HD) // HD
    rows = req_rows * groups
    slot_count, span = sk_ref.shape[0], sk_ref.shape[1]
    chunks = pk_ref.shape[0] // CHUNK

    def prefix_copies(i):
        at = pl.ds(i * CHUNK, CHUNK)
        return (
            pltpu.make_async_copy(pk_ref.at[at], kbuf.at[at], ksem.at[i]),
            pltpu.make_async_copy(pv_ref.at[at], vbuf.at[at], vsem.at[i]),
        )

    def suffix_copies(s):
        return (
            pltpu.make_async_copy(sk_ref.at[s], skbuf.at[s], ssem.at[0, s]),
            pltpu.make_async_copy(sv_ref.at[s], svbuf.at[s], ssem.at[1, s]),
        )

    for i in range(chunks):
        for copy in prefix_copies(i):
            copy.start()
    for s in range(slot_count):
        for copy in suffix_copies(s):
            copy.start()

    for g in range(groups):
        qrow[g * req_rows : (g + 1) * req_rows] = q_ref[:, g * HD : (g + 1) * HD]
    acc[...] = jnp.zeros_like(acc)
    total[...] = jnp.zeros_like(total)

    def chunk_step(i, unused):
        for copy in prefix_copies(i):
            copy.wait()

        @pl.when(i == 0)
        def _():
            for r in range(0, rows, TILE):
                s = dot_t(qrow[r : r + TILE], kbuf[0:TILE]) * scale
                top[r : r + TILE] = jnp.broadcast_to(jnp.max(s, axis=1, keepdims=True), (TILE, HD))

        shift = jnp.concatenate([top[...]] * (TILE // HD), axis=1)
        mix = None
        weight_sum = None
        for t in range(0, CHUNK, TILE):
            at = pl.ds(pl.multiple_of(i * CHUNK + t, TILE), TILE)
            p = jnp.exp2(dot_t(qrow[...], kbuf[at]) * scale - shift)
            part = dot(p.astype(bf16), vbuf[at])
            part_sum = sum(p[:, u : u + HD] for u in range(0, TILE, HD))
            mix = part if mix is None else mix + part
            weight_sum = part_sum if weight_sum is None else weight_sum + part_sum
        acc[...] += mix
        total[...] += weight_sum
        return 0

    lax.fori_loop(0, chunks, chunk_step, 0)
    total[...] = lane_sum(total[...])

    @pl.when(jnp.logical_not(jnp.max(total[...]) < SAFE_SUM))
    def _():
        def safe_rows(j, unused):
            at = pl.ds(pl.multiple_of(j * TILE, TILE), TILE)
            q = qrow[at]

            def safe_keys(i, carried):
                high, summed, mixed = carried
                keys = pl.ds(pl.multiple_of(i * TILE, TILE), TILE)
                s = dot_t(q, kbuf[keys]) * scale
                new = jnp.maximum(high, jnp.broadcast_to(jnp.max(s, axis=1, keepdims=True), high.shape))
                p = jnp.exp2(s - jnp.concatenate([new] * (TILE // HD), axis=1))
                decay = jnp.exp2(high - new)
                part = jnp.broadcast_to(jnp.sum(p, axis=1, keepdims=True), high.shape)
                return new, summed * decay + part, mixed * decay + dot(p.astype(bf16), vbuf[keys])

            zero = jnp.zeros((TILE, HD), f32)
            high, summed, mixed = lax.fori_loop(
                0, chunks * CHUNK // TILE, safe_keys, (zero + NEG_BIG, zero, zero)
            )
            top[at] = high
            total[at] = summed
            acc[at] = mixed
            return 0

        lax.fori_loop(0, rows // TILE, safe_rows, 0)

    tokens = 2
    pad = 16
    pick_row = lax.broadcasted_iota(jnp.int32, (pad, req_rows), 0)
    pick_col = lax.broadcasted_iota(jnp.int32, (pad, req_rows), 1)
    put_row = lax.broadcasted_iota(jnp.int32, (req_rows, pad), 0)
    put_col = lax.broadcasted_iota(jnp.int32, (req_rows, pad), 1)
    pick_at = jnp.full((pad, req_rows), -1, jnp.int32)
    put_at = jnp.full((req_rows, pad), -1, jnp.int32)
    for s in range(slot_count):
        row = slots_ref[s] * tokens
        pick_at = jnp.where(pick_row // tokens == s, row + pick_row % tokens, pick_at)
        put_at = jnp.where(put_col // tokens == s, row + put_col % tokens, put_at)
    pick = jnp.where(pick_at == pick_col, 1.0, 0.0).astype(bf16)
    put_f = jnp.where(put_at == put_row, 1.0, 0.0)
    put = put_f.astype(bf16)
    picked = dot(pick, q_ref[...])
    new_keys = picked[:, groups * HD : (groups + 1) * HD].astype(bf16)
    new_values = picked[:, (groups + 1) * HD :].astype(bf16)
    slot_rows = groups * tokens
    for s in range(slot_count):
        for g in range(groups):
            qslot[s * slot_rows + g * tokens : s * slot_rows + (g + 1) * tokens] = picked[
                s * tokens : (s + 1) * tokens, g * HD : (g + 1) * HD
            ]
    oslot[...] = jnp.zeros_like(oslot)
    lslot[...] = jnp.zeros_like(lslot)
    fresh_row = lax.broadcasted_iota(jnp.int32, (slot_rows, pad), 0)
    fresh_col = lax.broadcasted_iota(jnp.int32, (slot_rows, pad), 1)
    position = lax.broadcasted_iota(jnp.int32, (slot_rows, span), 1)
    for s in range(slot_count):
        for copy in suffix_copies(s):
            copy.wait()
    for s in range(slot_count):
        q = qslot[s * slot_rows : (s + 1) * slot_rows].astype(bf16)
        live = position < slots_ref[slot_count + s]
        causal = (fresh_col // tokens == s) & (fresh_col % tokens <= fresh_row % tokens)
        scores = jnp.where(live, dot_t(q, skbuf[s]) * scale, NEG_BIG)
        fresh = jnp.where(causal, dot_t(q, new_keys) * scale, NEG_BIG)
        high = jnp.maximum(jnp.max(scores, axis=1, keepdims=True), jnp.max(fresh, axis=1, keepdims=True))
        p = jnp.exp2(scores - high)
        fresh_p = jnp.exp2(fresh - high)
        summed = jnp.sum(p, axis=1, keepdims=True) + jnp.sum(fresh_p, axis=1, keepdims=True)
        mixed = dot(p.astype(bf16), svbuf[s]) + dot(fresh_p.astype(bf16), new_values)
        mixed = mixed / summed
        level = jnp.broadcast_to(high + jnp.log(summed) * LOG2E, mixed.shape)
        for g in range(groups):
            put_at_rows = slice(s * tokens, (s + 1) * tokens)
            lanes = slice(g * HD, (g + 1) * HD)
            oslot[put_at_rows, lanes] = mixed[g * tokens : (g + 1) * tokens]
            lslot[put_at_rows, lanes] = level[g * tokens : (g + 1) * tokens]

    suffix_mix = sum(dot(put, piece) for piece in pieces(oslot[...]))
    suffix_level = sum(dot(put, piece) for piece in pieces(lslot[...]))
    has_suffix = jnp.sum(put_f, axis=1, keepdims=True) > 0.5
    lane = lax.broadcasted_iota(jnp.int32, (req_rows, HD), 1)
    levels = jnp.zeros((req_rows, HD), f32)
    for g in range(groups):
        at = slice(g * req_rows, (g + 1) * req_rows)
        lanes = slice(g * HD, (g + 1) * HD)
        level = top[at] + jnp.log(total[at]) * LOG2E
        other = jnp.where(has_suffix, suffix_level[:, lanes], NEG_BIG)
        high = jnp.maximum(level, other)
        mine = jnp.exp2(level - high)
        theirs = jnp.exp2(other - high)
        summed = mine + theirs
        mixed = (acc[at] / total[at] * mine + suffix_mix[:, lanes] * theirs) / summed
        out_ref[:, lanes] = mixed.astype(bf16)
        level = high + jnp.log(summed) * LOG2E
        for j, piece in enumerate(pieces(level)):
            levels = jnp.where(lane == j * groups + g, piece.astype(f32), levels)
    out_ref[:, groups * HD :] = levels.astype(bf16)


def merge_kernel(sources, copies, part_ref, out_ref):
    rows = part_ref.shape[0]
    home_rows = rows // sources
    groups = (part_ref.shape[1] - HD) // HD
    levels = part_ref[:, groups * HD :].astype(f32)
    lane = lax.broadcasted_iota(jnp.int32, (rows, HD), 1)
    for g in range(groups):
        mine = (lane % groups == g) & (lane < 3 * groups)
        level = lane_sum(jnp.where(mine, levels, 0.0)).reshape(sources, home_rows, HD)
        weight = jnp.exp2(level - jnp.max(level, axis=0, keepdims=True))
        part = part_ref[:, g * HD : (g + 1) * HD].astype(f32).reshape(sources, home_rows, HD)
        mixed = jnp.sum(part * weight, axis=0) / jnp.sum(weight, axis=0)
        out_ref[:, g * HD : (g + 1) * HD] = jnp.concatenate([mixed] * copies, axis=0).astype(bf16)


def on_device(queries, prefix_k, prefix_v, suffix_k, suffix_v, new_k, new_v, suffix_len, owner_of):
    req_local, tokens, width = queries.shape
    groups = width // HD
    slot_count, span = suffix_k.shape[0], suffix_k.shape[1]
    ctx_count = lax.axis_size("ctx")
    head_count = lax.axis_size("head")
    ctx_index = lax.axis_index("ctx")
    home_rows = req_local * tokens
    all_rows = ctx_count * home_rows
    rows = all_rows * groups
    vmem = pl.BlockSpec(memory_space=pltpu.VMEM)
    smem = pl.BlockSpec(memory_space=pltpu.SMEM)
    hbm = pl.BlockSpec(memory_space=pl.ANY)

    sent = pl.pallas_call(
        functools.partial(spread_kernel, ctx_count),
        in_specs=[vmem] * 3,
        out_specs=vmem,
        out_shape=jax.ShapeDtypeStruct((all_rows, width + 2 * HD), bf16),
        name="spread",
    )(queries, new_k, new_v)
    gathered = lax.all_to_all(sent, "ctx", split_axis=0, concat_axis=0, tiled=True)

    my_slots = ctx_index * slot_count + jnp.arange(slot_count, dtype=jnp.int32)
    incoming = owner_of[None, :] == my_slots[:, None]
    request = jnp.arange(owner_of.shape[0], dtype=jnp.int32)
    slot_request = jnp.max(jnp.where(incoming, request[None, :], -4), axis=1)
    slot_length = jnp.sum(jnp.where(incoming, suffix_len[None, :], 0), axis=1)
    slots = jnp.concatenate([slot_request, slot_length])

    chunks = prefix_k.shape[0] // CHUNK
    parts = pl.pallas_call(
        functools.partial(attend_kernel, HD**-0.5 * LOG2E),
        in_specs=[smem, vmem, hbm, hbm, hbm, hbm],
        out_specs=vmem,
        out_shape=jax.ShapeDtypeStruct((all_rows, width + HD), bf16),
        scratch_shapes=[
            pltpu.VMEM(prefix_k.shape, bf16),
            pltpu.VMEM(prefix_v.shape, bf16),
            pltpu.VMEM(suffix_k.shape, bf16),
            pltpu.VMEM(suffix_v.shape, bf16),
            pltpu.VMEM((rows, HD), bf16),
            pltpu.VMEM((rows, HD), f32),
            pltpu.VMEM((rows, HD), f32),
            pltpu.VMEM((rows, HD), f32),
            pltpu.VMEM((slot_count * groups * tokens, HD), f32),
            pltpu.VMEM((16, width), f32),
            pltpu.VMEM((16, width), f32),
            pltpu.SemaphoreType.DMA((chunks,)),
            pltpu.SemaphoreType.DMA((chunks,)),
            pltpu.SemaphoreType.DMA((2, slot_count)),
        ],
        compiler_params=pltpu.CompilerParams(vmem_limit_bytes=56 * 1024 * 1024),
        name="attend",
    )(slots, gathered, prefix_k, prefix_v, suffix_k, suffix_v)
    arrived = lax.all_to_all(parts, "ctx", split_axis=0, concat_axis=0, tiled=True)

    finished = pl.pallas_call(
        functools.partial(merge_kernel, ctx_count, head_count),
        in_specs=[vmem],
        out_specs=vmem,
        out_shape=jax.ShapeDtypeStruct((head_count * home_rows, width), bf16),
        name="merge",
    )(arrived)
    heads = lax.all_to_all(finished, "head", split_axis=0, concat_axis=0, tiled=True)
    heads = heads.reshape(head_count, home_rows, width).transpose(1, 0, 2)
    return heads.reshape(req_local, tokens, head_count * width)


def solution(mesh):
    placed = (
        P("ctx", None, "head"),
        P("ctx", "head"),
        P("ctx", "head"),
        P("ctx", None, "head"),
        P("ctx", None, "head"),
        P("ctx", None, "head"),
        P("ctx", None, "head"),
        P(),
        P(),
    )
    return jax.shard_map(
        on_device, mesh=mesh, in_specs=placed, out_specs=P("ctx", None, None), check_vma=False
    )
```

```python
import functools

import jax
import jax.numpy as jnp
from jax import lax
from jax.experimental import pallas as pl
from jax.experimental.pallas import tpu as pltpu
from jax.sharding import PartitionSpec as P

H = 64
KV = 8
HD = 128
LOG2E = 1.4426950408889634
NEG_BIG = -1e30
SAFE_SUM = 2.0**60

TOKENS = 2
PAD = 16
CHUNK = 4096
TILE = 256
SUFFIX_AT = (1, 5, 9)

f32 = jnp.float32
bf16 = jnp.bfloat16


def dot(a, b):
    return lax.dot_general(a, b, (((1,), (0,)), ((), ())), preferred_element_type=f32)


def dot_t(a, b):
    return lax.dot_general(a, b, (((1,), (1,)), ((), ())), preferred_element_type=f32)


def lane_sum(x):
    return jnp.broadcast_to(jnp.sum(x, axis=1, keepdims=True), x.shape)


def pieces(x):
    first = x.astype(bf16)
    rest = x - first.astype(f32)
    second = rest.astype(bf16)
    third = (rest - second.astype(f32)).astype(bf16)
    return first, second, third


def spread_kernel(copies, q_ref, k_ref, v_ref, out_ref):
    rows = q_ref.shape[0] * q_ref.shape[1]
    width = q_ref.shape[2]
    block = jnp.concatenate(
        [
            q_ref[...].astype(f32).reshape(rows, width),
            k_ref[...].astype(f32).reshape(rows, HD),
            v_ref[...].astype(f32).reshape(rows, HD),
        ],
        axis=1,
    )
    out_ref[...] = jnp.concatenate([block] * copies, axis=0).astype(bf16)


def attend_kernel(
    scale, slots_ref, q_ref, pk_ref, pv_ref, sk_ref, sv_ref, out_ref,
    kbuf, vbuf, skbuf, svbuf, qrow, top, acc, total, qslot, oraw, lraw, oslot, lslot, ksem, vsem, ssem,
):
    req_rows = q_ref.shape[0]
    groups = (q_ref.shape[1] - 2 * HD) // HD
    rows = req_rows * groups
    slot_count, span = sk_ref.shape[0], sk_ref.shape[1]
    slot_rows = groups * TOKENS
    chunks = pk_ref.shape[0] // CHUNK
    per_step = slot_count // (chunks - 1)

    def prefix_copies(i):
        at = pl.ds(i * CHUNK, CHUNK)
        return (
            pltpu.make_async_copy(pk_ref.at[at], kbuf.at[at], ksem.at[i]),
            pltpu.make_async_copy(pv_ref.at[at], vbuf.at[at], vsem.at[i]),
        )

    def suffix_copies(s):
        return (
            pltpu.make_async_copy(sk_ref.at[s], skbuf.at[s], ssem.at[0, s]),
            pltpu.make_async_copy(sv_ref.at[s], svbuf.at[s], ssem.at[1, s]),
        )

    for copy in prefix_copies(0):
        copy.start()

    for g in range(groups):
        qrow[g * req_rows : (g + 1) * req_rows] = q_ref[:, g * HD : (g + 1) * HD]
    acc[...] = jnp.zeros_like(acc)
    total[...] = jnp.zeros_like(total)

    pick_row = lax.broadcasted_iota(jnp.int32, (PAD, req_rows), 0)
    pick_col = lax.broadcasted_iota(jnp.int32, (PAD, req_rows), 1)
    put_row = lax.broadcasted_iota(jnp.int32, (req_rows, PAD), 0)
    put_col = lax.broadcasted_iota(jnp.int32, (req_rows, PAD), 1)
    pick_at = jnp.full((PAD, req_rows), -1, jnp.int32)
    put_at = jnp.full((req_rows, PAD), -1, jnp.int32)
    for s in range(slot_count):
        row = slots_ref[s] * TOKENS
        pick_at = jnp.where(pick_row // TOKENS == s, row + pick_row % TOKENS, pick_at)
        put_at = jnp.where(put_col // TOKENS == s, row + put_col % TOKENS, put_at)
    pick = jnp.where(pick_at == pick_col, 1.0, 0.0).astype(bf16)
    picked = dot(pick, q_ref[...])
    new_keys = picked[:, groups * HD : (groups + 1) * HD].astype(bf16)
    new_values = picked[:, (groups + 1) * HD :].astype(bf16)
    for s in range(slot_count):
        for g in range(groups):
            qslot[s * slot_rows + g * TOKENS : s * slot_rows + (g + 1) * TOKENS] = picked[
                s * TOKENS : (s + 1) * TOKENS, g * HD : (g + 1) * HD
            ]
    fresh_row = lax.broadcasted_iota(jnp.int32, (slot_rows, PAD), 0)
    fresh_col = lax.broadcasted_iota(jnp.int32, (slot_rows, PAD), 1)
    position = lax.broadcasted_iota(jnp.int32, (slot_rows, span), 1)

    def suffix_stages(slots):
        held = {}
        count = len(slots)

        def blocks(make):
            return jnp.concatenate([make(s) for s in slots], axis=0)

        def apart(x):
            zero = jnp.zeros((slot_rows, HD), x.dtype)
            own = [x[n * slot_rows : (n + 1) * slot_rows] for n in range(count)]
            return jnp.concatenate(
                [jnp.concatenate([own[n] if m == n else zero for m in range(count)], axis=1) for n in range(count)],
                axis=0,
            )

        def score():
            q = blocks(lambda s: qslot[pl.ds(pl.multiple_of(s * slot_rows, slot_rows), slot_rows)])
            causal = blocks(
                lambda s: (fresh_col // TOKENS == s) & (fresh_col % TOKENS <= fresh_row % TOKENS)
            )
            live = blocks(lambda s: position < slots_ref[slot_count + s])
            keys = jnp.concatenate([skbuf[s] for s in slots], axis=1)
            held["scores"] = jnp.where(live, dot_t(apart(q).astype(bf16), keys) * scale, NEG_BIG)
            held["fresh"] = jnp.where(causal, dot_t(q.astype(bf16), new_keys) * scale, NEG_BIG)

        def weigh():
            scores, fresh = held["scores"], held["fresh"]
            high = jnp.maximum(
                jnp.max(scores, axis=1, keepdims=True), jnp.max(fresh, axis=1, keepdims=True)
            )
            p = jnp.exp2(scores - high)
            fresh_p = jnp.exp2(fresh - high)
            held["sum"] = jnp.sum(p, axis=1, keepdims=True) + jnp.sum(fresh_p, axis=1, keepdims=True)
            held["high"], held["p"], held["fresh_p"] = high, p.astype(bf16), fresh_p.astype(bf16)

        def mix():
            values = jnp.concatenate([svbuf[s] for s in slots], axis=1)
            wide = dot(held["p"], values)
            fresh_mix = dot(held["fresh_p"], new_values)
            level = held["high"] + jnp.log(held["sum"]) * LOG2E
            for n, s in enumerate(slots):
                at = slice(n * slot_rows, (n + 1) * slot_rows)
                mixed = wide[at, n * HD : (n + 1) * HD] + fresh_mix[at]
                oraw[s] = mixed / held["sum"][at]
                lraw[s] = jnp.broadcast_to(level[at], mixed.shape)

        return [score, weigh, mix]

    def chunk_step(i, slots):
        stages = {}
        for copy in prefix_copies(i):
            copy.wait()
        if slots:
            for s in slots:
                for copy in suffix_copies(s):
                    copy.wait()
            stages = dict(zip(SUFFIX_AT, suffix_stages(slots)))

        def start_next():
            for copy in prefix_copies(i + 1):
                copy.start()
            for n in range(per_step):
                for copy in suffix_copies(i * per_step + n):
                    copy.start()

        if slots:
            pl.when(i + 1 < chunks)(start_next)
        else:
            start_next()
            for r in range(0, rows, TILE):
                s = dot_t(qrow[r : r + TILE], kbuf[0:TILE]) * scale
                top[r : r + TILE] = jnp.broadcast_to(jnp.max(s, axis=1, keepdims=True), (TILE, HD))
        shift = jnp.concatenate([top[...]] * (TILE // HD), axis=1)
        mix = None
        weight_sum = None
        for n, t in enumerate(range(0, CHUNK, TILE)):
            at = pl.ds(pl.multiple_of(i * CHUNK + t, TILE), TILE)
            p = jnp.exp2(dot_t(qrow[...], kbuf[at]) * scale - shift)
            part = dot(p.astype(bf16), vbuf[at])
            part_sum = sum(p[:, u : u + HD] for u in range(0, TILE, HD))
            mix = part if mix is None else mix + part
            weight_sum = part_sum if weight_sum is None else weight_sum + part_sum
            if n in stages:
                stages[n]()
        acc[...] += mix
        total[...] += weight_sum

    chunk_step(0, ())

    def later_step(i, unused):
        chunk_step(i, [(i - 1) * per_step + n for n in range(per_step)])
        return 0

    lax.fori_loop(1, chunks, later_step, 0)
    total[...] = lane_sum(total[...])

    @pl.when(jnp.logical_not(jnp.max(total[...]) < SAFE_SUM))
    def _():
        def safe_rows(j, unused):
            at = pl.ds(pl.multiple_of(j * TILE, TILE), TILE)
            q = qrow[at]

            def safe_keys(i, carried):
                high, summed, mixed = carried
                keys = pl.ds(pl.multiple_of(i * TILE, TILE), TILE)
                s = dot_t(q, kbuf[keys]) * scale
                new = jnp.maximum(high, jnp.broadcast_to(jnp.max(s, axis=1, keepdims=True), high.shape))
                p = jnp.exp2(s - jnp.concatenate([new] * (TILE // HD), axis=1))
                decay = jnp.exp2(high - new)
                part = jnp.broadcast_to(jnp.sum(p, axis=1, keepdims=True), high.shape)
                return new, summed * decay + part, mixed * decay + dot(p.astype(bf16), vbuf[keys])

            zero = jnp.zeros((TILE, HD), f32)
            high, summed, mixed = lax.fori_loop(
                0, chunks * CHUNK // TILE, safe_keys, (zero + NEG_BIG, zero, zero)
            )
            top[at] = high
            total[at] = summed
            acc[at] = mixed
            return 0

        lax.fori_loop(0, rows // TILE, safe_rows, 0)

    oslot[...] = jnp.zeros_like(oslot)
    lslot[...] = jnp.zeros_like(lslot)
    for s in range(slot_count):
        for g in range(groups):
            put_rows = slice(s * TOKENS, (s + 1) * TOKENS)
            lanes = slice(g * HD, (g + 1) * HD)
            oslot[put_rows, lanes] = oraw[s, g * TOKENS : (g + 1) * TOKENS]
            lslot[put_rows, lanes] = lraw[s, g * TOKENS : (g + 1) * TOKENS]
    put_f = jnp.where(put_at == put_row, 1.0, 0.0)
    put = put_f.astype(bf16)
    suffix_mix = sum(dot(put, piece) for piece in pieces(oslot[...]))
    suffix_level = sum(dot(put, piece) for piece in pieces(lslot[...]))
    has_suffix = jnp.sum(put_f, axis=1, keepdims=True) > 0.5
    lane = lax.broadcasted_iota(jnp.int32, (req_rows, HD), 1)
    levels = jnp.zeros((req_rows, HD), f32)
    for g in range(groups):
        at = slice(g * req_rows, (g + 1) * req_rows)
        lanes = slice(g * HD, (g + 1) * HD)
        level = top[at] + jnp.log(total[at]) * LOG2E
        other = jnp.where(has_suffix, suffix_level[:, lanes], NEG_BIG)
        high = jnp.maximum(level, other)
        mine = jnp.exp2(level - high)
        theirs = jnp.exp2(other - high)
        summed = mine + theirs
        mixed = (acc[at] / total[at] * mine + suffix_mix[:, lanes] * theirs) / summed
        out_ref[:, lanes] = mixed.astype(bf16)
        level = high + jnp.log(summed) * LOG2E
        for j, piece in enumerate(pieces(level)):
            levels = jnp.where(lane == j * groups + g, piece.astype(f32), levels)
    out_ref[:, groups * HD :] = levels.astype(bf16)


def attend(slots, gathered, prefix_k, prefix_v, suffix_k, suffix_v):
    all_rows = gathered.shape[0]
    width = gathered.shape[1] - 2 * HD
    groups = width // HD
    rows = all_rows * groups
    slot_count = suffix_k.shape[0]
    slot_rows = groups * TOKENS
    chunks = prefix_k.shape[0] // CHUNK
    vmem = pl.BlockSpec(memory_space=pltpu.VMEM)
    smem = pl.BlockSpec(memory_space=pltpu.SMEM)
    hbm = pl.BlockSpec(memory_space=pl.ANY)
    return pl.pallas_call(
        functools.partial(attend_kernel, HD**-0.5 * LOG2E),
        in_specs=[smem, vmem, hbm, hbm, hbm, hbm],
        out_specs=vmem,
        out_shape=pltpu.VMEM((all_rows, width + HD), bf16),
        scratch_shapes=[
            pltpu.VMEM(prefix_k.shape, bf16),
            pltpu.VMEM(prefix_v.shape, bf16),
            pltpu.VMEM(suffix_k.shape, bf16),
            pltpu.VMEM(suffix_v.shape, bf16),
            pltpu.VMEM((rows, HD), bf16),
            pltpu.VMEM((rows, HD), f32),
            pltpu.VMEM((rows, HD), f32),
            pltpu.VMEM((rows, HD), f32),
            pltpu.VMEM((slot_count * slot_rows, HD), f32),
            pltpu.VMEM((slot_count, slot_rows, HD), f32),
            pltpu.VMEM((slot_count, slot_rows, HD), f32),
            pltpu.VMEM((PAD, width), f32),
            pltpu.VMEM((PAD, width), f32),
            pltpu.SemaphoreType.DMA((chunks,)),
            pltpu.SemaphoreType.DMA((chunks,)),
            pltpu.SemaphoreType.DMA((2, slot_count)),
        ],
        compiler_params=pltpu.CompilerParams(vmem_limit_bytes=56 * 1024 * 1024),
        name="attend",
    )(slots, pltpu.with_memory_space_constraint(gathered, pltpu.VMEM), prefix_k, prefix_v, suffix_k, suffix_v)


def merge_kernel(sources, copies, part_ref, out_ref):
    rows = part_ref.shape[0]
    home_rows = rows // sources
    groups = (part_ref.shape[1] - HD) // HD
    levels = part_ref[:, groups * HD :].astype(f32)
    lane = lax.broadcasted_iota(jnp.int32, (rows, HD), 1)
    for g in range(groups):
        mine = (lane % groups == g) & (lane < 3 * groups)
        level = lane_sum(jnp.where(mine, levels, 0.0)).reshape(sources, home_rows, HD)
        weight = jnp.exp2(level - jnp.max(level, axis=0, keepdims=True))
        part = part_ref[:, g * HD : (g + 1) * HD].astype(f32).reshape(sources, home_rows, HD)
        mixed = jnp.sum(part * weight, axis=0) / jnp.sum(weight, axis=0)
        out_ref[:, g * HD : (g + 1) * HD] = jnp.concatenate([mixed] * copies, axis=0).astype(bf16)


def on_device(queries, prefix_k, prefix_v, suffix_k, suffix_v, new_k, new_v, suffix_len, owner_of):
    req_local, tokens, width = queries.shape
    groups = width // HD
    slot_count, span = suffix_k.shape[0], suffix_k.shape[1]
    ctx_count = lax.axis_size("ctx")
    head_count = lax.axis_size("head")
    ctx_index = lax.axis_index("ctx")
    home_rows = req_local * tokens
    all_rows = ctx_count * home_rows
    rows = all_rows * groups
    vmem = pl.BlockSpec(memory_space=pltpu.VMEM)

    sent = pl.pallas_call(
        functools.partial(spread_kernel, ctx_count),
        in_specs=[vmem] * 3,
        out_specs=vmem,
        out_shape=pltpu.VMEM((all_rows, width + 2 * HD), bf16),
        name="spread",
    )(queries, new_k, new_v)
    gathered = lax.all_to_all(sent, "ctx", split_axis=0, concat_axis=0, tiled=True)

    my_slots = ctx_index * slot_count + jnp.arange(slot_count, dtype=jnp.int32)
    incoming = owner_of[None, :] == my_slots[:, None]
    request = jnp.arange(owner_of.shape[0], dtype=jnp.int32)
    slot_request = jnp.max(jnp.where(incoming, request[None, :], -4), axis=1)
    slot_length = jnp.sum(jnp.where(incoming, suffix_len[None, :], 0), axis=1)
    slots = jnp.concatenate([slot_request, slot_length])

    parts = attend(slots, gathered, prefix_k, prefix_v, suffix_k, suffix_v)
    arrived = lax.all_to_all(parts, "ctx", split_axis=0, concat_axis=0, tiled=True)

    finished = pl.pallas_call(
        functools.partial(merge_kernel, ctx_count, head_count),
        in_specs=[vmem],
        out_specs=vmem,
        out_shape=pltpu.VMEM((head_count * home_rows, width), bf16),
        name="merge",
    )(pltpu.with_memory_space_constraint(arrived, pltpu.VMEM))
    heads = lax.all_to_all(finished, "head", split_axis=0, concat_axis=0, tiled=True)
    heads = heads.reshape(head_count, home_rows, width).transpose(1, 0, 2)
    return heads.reshape(req_local, tokens, head_count * width)


def solution(mesh):
    placed = (
        P("ctx", None, "head"),
        P("ctx", "head"),
        P("ctx", "head"),
        P("ctx", None, "head"),
        P("ctx", None, "head"),
        P("ctx", None, "head"),
        P("ctx", None, "head"),
        P(),
        P(),
    )
    return jax.shard_map(
        on_device, mesh=mesh, in_specs=placed, out_specs=P("ctx", None, None), check_vma=False
    )
```

```python
import functools

import jax
import jax.numpy as jnp
from jax import lax
from jax.experimental import pallas as pl
from jax.experimental.pallas import tpu as pltpu
from jax.sharding import PartitionSpec as P

H = 64
KV = 8
HD = 128
LOG2E = 1.4426950408889634
NEG_BIG = -1e30
SAFE_SUM = 2.0**60

TOKENS = 2
PAD = 16
CHUNK = 4096
TILE = 256
ROWBLK = 256
KEYBLK = 1024

f32 = jnp.float32
bf16 = jnp.bfloat16


def dot(a, b):
    return lax.dot_general(a, b, (((1,), (0,)), ((), ())), preferred_element_type=f32)


def dot_t(a, b):
    return lax.dot_general(a, b, (((1,), (1,)), ((), ())), preferred_element_type=f32)


def near(x):
    return pltpu.with_memory_space_constraint(x, pltpu.VMEM)


def lane_sum(x):
    return jnp.broadcast_to(jnp.sum(x, axis=1, keepdims=True), x.shape)


def pieces(x):
    first = x.astype(bf16)
    rest = x - first.astype(f32)
    second = rest.astype(bf16)
    third = (rest - second.astype(f32)).astype(bf16)
    return first, second, third


def spread_kernel(copies, q_ref, k_ref, v_ref, owner_ref, length_ref, out_ref, table_ref):
    rows = q_ref.shape[0] * q_ref.shape[1]
    width = q_ref.shape[2]
    block = jnp.concatenate(
        [
            q_ref[...].astype(f32).reshape(rows, width),
            k_ref[...].astype(f32).reshape(rows, HD),
            v_ref[...].astype(f32).reshape(rows, HD),
        ],
        axis=1,
    )
    out_ref[...] = jnp.concatenate([block] * copies, axis=0).astype(bf16)
    table_ref[0:1] = owner_ref[...]
    table_ref[1:2] = length_ref[...]


def attend_kernel(
    scale, table_ref, q_ref, pk_ref, pv_ref, sk_ref, sv_ref, out_ref,
    kbuf, vbuf, vturn, skbuf, svbuf, qrow, top, acc, total, qslot, oraw, lraw, oslot, lslot, ksem, vsem, ssem,
):
    req_rows = q_ref.shape[0]
    groups = (q_ref.shape[1] - 2 * HD) // HD
    rows = req_rows * groups
    slot_count, span = sk_ref.shape[0], sk_ref.shape[1]
    slot_rows = groups * TOKENS
    chunks = pk_ref.shape[0] // CHUNK
    per_step = slot_count // (chunks - 1)

    def prefix_copies(i):
        at = pl.ds(i * CHUNK, CHUNK)
        return (
            pltpu.make_async_copy(pk_ref.at[at], kbuf.at[at], ksem.at[i]),
            pltpu.make_async_copy(pv_ref.at[at], vbuf.at[at], vsem.at[i]),
        )

    def suffix_copies(s):
        return (
            pltpu.make_async_copy(sk_ref.at[s], skbuf.at[s], ssem.at[0, s]),
            pltpu.make_async_copy(sv_ref.at[s], svbuf.at[s], ssem.at[1, s]),
        )

    for copy in prefix_copies(0):
        copy.start()

    for g in range(groups):
        qrow[g * req_rows : (g + 1) * req_rows] = q_ref[:, g * HD : (g + 1) * HD]
    acc[...] = jnp.zeros_like(acc)
    total[...] = jnp.zeros_like(total)

    requests = table_ref.shape[1]
    base = lax.axis_index("ctx") * slot_count
    slot_of = lax.broadcasted_iota(jnp.int32, (PAD, requests), 0) // TOKENS
    owned = (table_ref[0:1] == base + slot_of) & (slot_of < slot_count)
    lengths = jnp.sum(jnp.where(owned, table_ref[1:2], 0), axis=1, keepdims=True)
    spread_row = lax.broadcasted_iota(jnp.int32, (requests, req_rows), 0)
    spread_col = lax.broadcasted_iota(jnp.int32, (requests, req_rows), 1)
    spread = jnp.where(spread_col // TOKENS == spread_row, 1.0, 0.0).astype(bf16)
    pick_row = lax.broadcasted_iota(jnp.int32, (PAD, req_rows), 0)
    pick_col = lax.broadcasted_iota(jnp.int32, (PAD, req_rows), 1)
    pick = dot(jnp.where(owned, 1.0, 0.0).astype(bf16), spread)
    pick = jnp.where(pick_row % TOKENS == pick_col % TOKENS, pick, 0.0).astype(bf16)
    picked = dot(pick, q_ref[...])
    new_keys = picked[:, groups * HD : (groups + 1) * HD].astype(bf16)
    new_values = picked[:, (groups + 1) * HD :].astype(bf16)
    for s in range(slot_count):
        for g in range(groups):
            qslot[s * slot_rows + g * TOKENS : s * slot_rows + (g + 1) * TOKENS] = picked[
                s * TOKENS : (s + 1) * TOKENS, g * HD : (g + 1) * HD
            ]
    fresh_row = lax.broadcasted_iota(jnp.int32, (slot_rows, PAD), 0)
    fresh_col = lax.broadcasted_iota(jnp.int32, (slot_rows, PAD), 1)
    position = lax.broadcasted_iota(jnp.int32, (slot_rows, span), 1)

    def suffix_stages(slots):
        held = {}
        count = len(slots)

        def blocks(make):
            return jnp.concatenate([make(s) for s in slots], axis=0)

        def apart(x):
            zero = jnp.zeros((slot_rows, HD), x.dtype)
            own = [x[n * slot_rows : (n + 1) * slot_rows] for n in range(count)]
            return jnp.concatenate(
                [jnp.concatenate([own[n] if m == n else zero for m in range(count)], axis=1) for n in range(count)],
                axis=0,
            )

        def score():
            q = blocks(lambda s: qslot[pl.ds(pl.multiple_of(s * slot_rows, slot_rows), slot_rows)])
            causal = blocks(
                lambda s: (fresh_col // TOKENS == s) & (fresh_col % TOKENS <= fresh_row % TOKENS)
            )
            live = blocks(lambda s: position < lengths[s * TOKENS : s * TOKENS + 1])
            keys = jnp.concatenate([skbuf[s] for s in slots], axis=1)
            held["scores"] = jnp.where(live, dot_t(apart(q).astype(bf16), keys) * scale, NEG_BIG)
            held["fresh"] = jnp.where(causal, dot_t(q.astype(bf16), new_keys) * scale, NEG_BIG)

        def weigh():
            scores, fresh = held["scores"], held["fresh"]
            high = jnp.maximum(
                jnp.max(scores, axis=1, keepdims=True), jnp.max(fresh, axis=1, keepdims=True)
            )
            p = jnp.exp2(scores - high)
            fresh_p = jnp.exp2(fresh - high)
            held["sum"] = jnp.sum(p, axis=1, keepdims=True) + jnp.sum(fresh_p, axis=1, keepdims=True)
            held["high"], held["p"], held["fresh_p"] = high, p.astype(bf16), fresh_p.astype(bf16)

        def mix():
            values = jnp.concatenate([svbuf[s] for s in slots], axis=1)
            wide = dot(held["p"], values)
            fresh_mix = dot(held["fresh_p"], new_values)
            level = held["high"] + jnp.log(held["sum"]) * LOG2E
            for n, s in enumerate(slots):
                at = slice(n * slot_rows, (n + 1) * slot_rows)
                mixed = wide[at, n * HD : (n + 1) * HD] + fresh_mix[at]
                oraw[s] = mixed / held["sum"][at]
                lraw[s] = jnp.broadcast_to(level[at], mixed.shape)

        return [score, weigh, mix]

    def first_top():
        for r in range(0, rows, ROWBLK):
            high = jnp.max(dot_t(kbuf[0:TILE], qrow[r : r + ROWBLK]), axis=0, keepdims=True) * scale
            top[:, r : r + ROWBLK] = jnp.broadcast_to(high, (8, ROWBLK))

    def start_next(i):
        for copy in prefix_copies(i + 1):
            copy.start()
        for n in range(per_step):
            for copy in suffix_copies(i * per_step + n):
                copy.start()

    def wait_suffix(i):
        for n in range(per_step):
            for copy in suffix_copies(i * per_step + n):
                copy.wait()

    def prefix_chunk(i):
        vturn[...] = jnp.transpose(vbuf[pl.ds(pl.multiple_of(i * CHUNK, CHUNK), CHUNK)])
        blocks = [(r, t) for r in range(0, rows, ROWBLK) for t in range(0, CHUNK, KEYBLK)]

        def score(block):
            r, t = block
            keys = pl.ds(pl.multiple_of(i * CHUNK + t, KEYBLK), KEYBLK)
            return dot_t(kbuf[keys], qrow[r : r + ROWBLK])

        ready = score(blocks[0])
        mix = weight_sum = None
        for n, (r, t) in enumerate(blocks):
            scores = ready
            if n + 1 < len(blocks):
                ready = score(blocks[n + 1])
            p = jnp.exp2(scores * scale - top[0:1, r : r + ROWBLK])
            part = dot(vturn[:, t : t + KEYBLK], p.astype(bf16))
            part_sum = jnp.sum(p.reshape(KEYBLK // 8, 8, ROWBLK), axis=0)
            mix = part if t == 0 else mix + part
            weight_sum = part_sum if t == 0 else weight_sum + part_sum
            if t + KEYBLK == CHUNK:
                acc[:, r : r + ROWBLK] += mix
                total[:, r : r + ROWBLK] += weight_sum

    def step(i, unused):
        keys_copy, values_copy = prefix_copies(i)
        keys_copy.wait()
        pl.when(i + 1 < chunks)(lambda: start_next(i))
        pl.when(i == 0)(first_top)
        values_copy.wait()
        prefix_chunk(i)
        return 0

    lax.fori_loop(0, chunks, step, 0)
    summed = jnp.sum(total[...], axis=0, keepdims=True)
    total[...] = jnp.broadcast_to(summed, total.shape)

    @pl.when(jnp.logical_not(jnp.max(summed) < SAFE_SUM))
    def _():
        def safe_rows(j, unused):
            at = pl.ds(pl.multiple_of(j * ROWBLK, ROWBLK), ROWBLK)
            q = qrow[at]

            def safe_keys(i, carried):
                high, summed, mixed = carried
                keys = pl.ds(pl.multiple_of(i * TILE, TILE), TILE)
                s = dot_t(kbuf[keys], q) * scale
                new = jnp.maximum(high, jnp.max(s, axis=0, keepdims=True))
                p = jnp.exp2(s - new)
                decay = jnp.exp2(high - new)
                summed = summed * decay + jnp.sum(p, axis=0, keepdims=True)
                return new, summed, mixed * decay + dot(jnp.transpose(vbuf[keys]), p.astype(bf16))

            zero = jnp.zeros((1, ROWBLK), f32)
            high, summed, mixed = lax.fori_loop(
                0, chunks * CHUNK // TILE, safe_keys, (zero + NEG_BIG, zero, jnp.zeros((HD, ROWBLK), f32))
            )
            top[:, at] = jnp.broadcast_to(high, (8, ROWBLK))
            total[:, at] = jnp.broadcast_to(summed, (8, ROWBLK))
            acc[:, at] = mixed
            return 0

        lax.fori_loop(0, rows // ROWBLK, safe_rows, 0)

    for i in range(chunks - 1):
        wait_suffix(i)
    staged = [suffix_stages([i * per_step + n for n in range(per_step)]) for i in range(chunks - 1)]
    for m in range(3):
        for stages in staged:
            stages[m]()
    oslot[...] = jnp.zeros_like(oslot)
    lslot[...] = jnp.zeros_like(lslot)
    for s in range(slot_count):
        for g in range(groups):
            put_rows = slice(s * TOKENS, (s + 1) * TOKENS)
            lanes = slice(g * HD, (g + 1) * HD)
            oslot[put_rows, lanes] = oraw[s, g * TOKENS : (g + 1) * TOKENS]
            lslot[put_rows, lanes] = lraw[s, g * TOKENS : (g + 1) * TOKENS]
    same_row = lax.broadcasted_iota(jnp.int32, (req_rows, req_rows), 0)
    same_col = lax.broadcasted_iota(jnp.int32, (req_rows, req_rows), 1)
    put_f = dot_t(jnp.where(same_row == same_col, 1.0, 0.0).astype(bf16), pick)
    put = put_f.astype(bf16)
    suffix_mix = sum(dot(put, piece) for piece in pieces(oslot[...]))
    suffix_level = sum(dot(put, piece) for piece in pieces(lslot[...]))
    has_suffix = jnp.sum(put_f, axis=1, keepdims=True) > 0.5
    lane = lax.broadcasted_iota(jnp.int32, (req_rows, HD), 1)
    levels = jnp.zeros((req_rows, HD), f32)
    for g in range(groups):
        at = slice(g * req_rows, (g + 1) * req_rows)
        lanes = slice(g * HD, (g + 1) * HD)
        level = top[0:1, at] + jnp.log(total[0:1, at]) * LOG2E
        level = jnp.transpose(jnp.broadcast_to(level, (HD, req_rows)))
        prefix_mix = jnp.transpose(acc[:, at] / total[0:1, at])
        other = jnp.where(has_suffix, suffix_level[:, lanes], NEG_BIG)
        high = jnp.maximum(level, other)
        mine = jnp.exp2(level - high)
        theirs = jnp.exp2(other - high)
        summed = mine + theirs
        mixed = (prefix_mix * mine + suffix_mix[:, lanes] * theirs) / summed
        out_ref[:, lanes] = mixed.astype(bf16)
        level = high + jnp.log(summed) * LOG2E
        for j, piece in enumerate(pieces(level)):
            levels = jnp.where(lane == j * groups + g, piece.astype(f32), levels)
    out_ref[:, groups * HD :] = levels.astype(bf16)


def attend(table, gathered, prefix_k, prefix_v, suffix_k, suffix_v):
    all_rows = gathered.shape[0]
    width = gathered.shape[1] - 2 * HD
    groups = width // HD
    rows = all_rows * groups
    slot_count = suffix_k.shape[0]
    slot_rows = groups * TOKENS
    chunks = prefix_k.shape[0] // CHUNK
    vmem = pl.BlockSpec(memory_space=pltpu.VMEM)
    hbm = pl.BlockSpec(memory_space=pl.ANY)
    return pl.pallas_call(
        functools.partial(attend_kernel, HD**-0.5 * LOG2E),
        in_specs=[vmem, vmem, hbm, hbm, hbm, hbm],
        out_specs=vmem,
        out_shape=pltpu.VMEM((all_rows, width + HD), bf16),
        scratch_shapes=[
            pltpu.VMEM(prefix_k.shape, bf16),
            pltpu.VMEM(prefix_v.shape, bf16),
            pltpu.VMEM((HD, CHUNK), bf16),
            pltpu.VMEM(suffix_k.shape, bf16),
            pltpu.VMEM(suffix_v.shape, bf16),
            pltpu.VMEM((rows, HD), bf16),
            pltpu.VMEM((8, rows), f32),
            pltpu.VMEM((HD, rows), f32),
            pltpu.VMEM((8, rows), f32),
            pltpu.VMEM((slot_count * slot_rows, HD), f32),
            pltpu.VMEM((slot_count, slot_rows, HD), f32),
            pltpu.VMEM((slot_count, slot_rows, HD), f32),
            pltpu.VMEM((PAD, width), f32),
            pltpu.VMEM((PAD, width), f32),
            pltpu.SemaphoreType.DMA((chunks,)),
            pltpu.SemaphoreType.DMA((chunks,)),
            pltpu.SemaphoreType.DMA((2, slot_count)),
        ],
        compiler_params=pltpu.CompilerParams(vmem_limit_bytes=56 * 1024 * 1024),
        name="attend",
    )(
        near(table),
        near(gathered),
        prefix_k,
        prefix_v,
        suffix_k,
        suffix_v,
    )


def merge_kernel(sources, copies, part_ref, out_ref):
    rows = part_ref.shape[0]
    home_rows = rows // sources
    groups = (part_ref.shape[1] - HD) // HD
    levels = part_ref[:, groups * HD :].astype(f32)
    lane = lax.broadcasted_iota(jnp.int32, (rows, HD), 1)
    for g in range(groups):
        mine = (lane % groups == g) & (lane < 3 * groups)
        level = lane_sum(jnp.where(mine, levels, 0.0)).reshape(sources, home_rows, HD)
        weight = jnp.exp2(level - jnp.max(level, axis=0, keepdims=True))
        part = part_ref[:, g * HD : (g + 1) * HD].astype(f32).reshape(sources, home_rows, HD)
        mixed = jnp.sum(part * weight, axis=0) / jnp.sum(weight, axis=0)
        out_ref[:, g * HD : (g + 1) * HD] = jnp.concatenate([mixed] * copies, axis=0).astype(bf16)


def on_device(queries, prefix_k, prefix_v, suffix_k, suffix_v, new_k, new_v, suffix_len, owner_of):
    req_local, tokens, width = queries.shape
    groups = width // HD
    ctx_count = lax.axis_size("ctx")
    head_count = lax.axis_size("head")
    home_rows = req_local * tokens
    all_rows = ctx_count * home_rows
    rows = all_rows * groups
    vmem = pl.BlockSpec(memory_space=pltpu.VMEM)

    sent, table = pl.pallas_call(
        functools.partial(spread_kernel, ctx_count),
        in_specs=[vmem] * 5,
        out_specs=[vmem] * 2,
        out_shape=[
            pltpu.VMEM((all_rows, width + 2 * HD), bf16),
            pltpu.VMEM((2, owner_of.shape[0]), jnp.int32),
        ],
        name="spread",
    )(queries, new_k, new_v, owner_of.reshape(1, -1), suffix_len.reshape(1, -1))
    gathered = lax.all_to_all(sent, "ctx", split_axis=0, concat_axis=0, tiled=True)

    parts = attend(table, gathered, prefix_k, prefix_v, suffix_k, suffix_v)
    arrived = lax.all_to_all(parts, "ctx", split_axis=0, concat_axis=0, tiled=True)

    finished = pl.pallas_call(
        functools.partial(merge_kernel, ctx_count, head_count),
        in_specs=[vmem],
        out_specs=vmem,
        out_shape=pltpu.VMEM((head_count * home_rows, width), bf16),
        name="merge",
    )(near(arrived))
    heads = lax.all_to_all(finished, "head", split_axis=0, concat_axis=0, tiled=True)
    heads = heads.reshape(head_count, home_rows, width).transpose(1, 0, 2)
    return heads.reshape(req_local, tokens, head_count * width)


def solution(mesh):
    placed = (
        P("ctx", None, "head"),
        P("ctx", "head"),
        P("ctx", "head"),
        P("ctx", None, "head"),
        P("ctx", None, "head"),
        P("ctx", None, "head"),
        P("ctx", None, "head"),
        P(),
        P(),
    )
    return jax.shard_map(
        on_device, mesh=mesh, in_specs=placed, out_specs=P("ctx", None, None), check_vma=False
    )
```

```python
import functools

import jax
import jax.numpy as jnp
from jax import lax
from jax.experimental import pallas as pl
from jax.experimental.pallas import tpu as pltpu
from jax.sharding import PartitionSpec as P

H = 64
KV = 8
HD = 128
LOG2E = 1.4426950408889634
NEG_BIG = -1e30
SAFE_SUM = 2.0**60

TOKENS = 2
PAD = 16
CHUNK = 4096
TILE = 256
ROWBLK = 256
KEYBLK = 1024

f32 = jnp.float32
bf16 = jnp.bfloat16


def dot(a, b):
    return lax.dot_general(a, b, (((1,), (0,)), ((), ())), preferred_element_type=f32)


def dot_t(a, b):
    return lax.dot_general(a, b, (((1,), (1,)), ((), ())), preferred_element_type=f32)


def near(x):
    return pltpu.with_memory_space_constraint(x, pltpu.VMEM)


def lane_sum(x):
    return jnp.broadcast_to(jnp.sum(x, axis=1, keepdims=True), x.shape)


def pieces(x):
    first = x.astype(bf16)
    rest = x - first.astype(f32)
    second = rest.astype(bf16)
    third = (rest - second.astype(f32)).astype(bf16)
    return first, second, third


def previous_row(x):
    return jnp.concatenate([x[-1:], x[:-1]], axis=0)


def spread_kernel(copies, q_ref, k_ref, v_ref, owner_ref, length_ref, out_ref, home_ref, table_ref):
    rows = q_ref.shape[0] * q_ref.shape[1]
    width = q_ref.shape[2]
    block = q_ref[...].astype(f32).reshape(rows, width)
    out_ref[...] = jnp.concatenate([block] * copies, axis=0).astype(bf16)
    home_ref[:, :width] = block
    home_ref[:, width : width + HD] = k_ref[...].astype(f32).reshape(rows, HD)
    home_ref[:, width + HD :] = v_ref[...].astype(f32).reshape(rows, HD)
    table_ref[0:1] = owner_ref[...]
    table_ref[1:2] = length_ref[...]


def attend_kernel(
    scale, table_ref, home_ref, q_ref, pk_ref, pv_ref, sk_ref, sv_ref, out_ref, fresh_ref,
    kbuf, vbuf, vturn, skbuf, svbuf, qrow, top, acc, total, qslot, oraw, lraw, oslot, lslot, ksem, vsem, ssem,
):
    req_rows = q_ref.shape[0]
    groups = q_ref.shape[1] // HD
    rows = req_rows * groups
    slot_count, span = sk_ref.shape[0], sk_ref.shape[1]
    slot_rows = groups * TOKENS
    chunks = pk_ref.shape[0] // CHUNK
    per_step = slot_count // (chunks - 1)

    def prefix_copies(i):
        at = pl.ds(i * CHUNK, CHUNK)
        return (
            pltpu.make_async_copy(pk_ref.at[at], kbuf.at[at], ksem.at[i]),
            pltpu.make_async_copy(pv_ref.at[at], vbuf.at[at], vsem.at[i]),
        )

    def suffix_copies(s):
        return (
            pltpu.make_async_copy(sk_ref.at[s], skbuf.at[s], ssem.at[0, s]),
            pltpu.make_async_copy(sv_ref.at[s], svbuf.at[s], ssem.at[1, s]),
        )

    for copy in prefix_copies(0):
        copy.start()

    for g in range(groups):
        qrow[g * req_rows : (g + 1) * req_rows] = q_ref[:, g * HD : (g + 1) * HD]
    acc[...] = jnp.zeros_like(acc)
    total[...] = jnp.zeros_like(total)

    key = home_ref[:, groups * HD : (groups + 1) * HD]
    second = lax.broadcasted_iota(jnp.int32, key.shape, 0) % TOKENS == 1
    for g in range(groups):
        q = home_ref[:, g * HD : (g + 1) * HD]
        fresh_ref[:, g * HD : (g + 1) * HD] = lane_sum(q * key) * scale
        first = lane_sum(q * previous_row(key)) * scale
        fresh_ref[:, (groups + g) * HD : (groups + g + 1) * HD] = jnp.where(second, first, NEG_BIG)

    requests = table_ref.shape[1]
    base = lax.axis_index("ctx") * slot_count
    slot_of = lax.broadcasted_iota(jnp.int32, (PAD, requests), 0) // TOKENS
    owned = (table_ref[0:1] == base + slot_of) & (slot_of < slot_count)
    lengths = jnp.sum(jnp.where(owned, table_ref[1:2], 0), axis=1, keepdims=True)
    spread_row = lax.broadcasted_iota(jnp.int32, (requests, req_rows), 0)
    spread_col = lax.broadcasted_iota(jnp.int32, (requests, req_rows), 1)
    spread = jnp.where(spread_col // TOKENS == spread_row, 1.0, 0.0).astype(bf16)
    pick_row = lax.broadcasted_iota(jnp.int32, (PAD, req_rows), 0)
    pick_col = lax.broadcasted_iota(jnp.int32, (PAD, req_rows), 1)
    pick = dot(jnp.where(owned, 1.0, 0.0).astype(bf16), spread)
    pick = jnp.where(pick_row % TOKENS == pick_col % TOKENS, pick, 0.0).astype(bf16)
    picked = dot(pick, q_ref[...])
    for s in range(slot_count):
        for g in range(groups):
            qslot[s * slot_rows + g * TOKENS : s * slot_rows + (g + 1) * TOKENS] = picked[
                s * TOKENS : (s + 1) * TOKENS, g * HD : (g + 1) * HD
            ]
    position = lax.broadcasted_iota(jnp.int32, (slot_rows, span), 1)

    def suffix_stages(slots):
        held = {}
        count = len(slots)

        def blocks(make):
            return jnp.concatenate([make(s) for s in slots], axis=0)

        def apart(x):
            zero = jnp.zeros((slot_rows, HD), x.dtype)
            own = [x[n * slot_rows : (n + 1) * slot_rows] for n in range(count)]
            return jnp.concatenate(
                [jnp.concatenate([own[n] if m == n else zero for m in range(count)], axis=1) for n in range(count)],
                axis=0,
            )

        def score():
            q = blocks(lambda s: qslot[pl.ds(pl.multiple_of(s * slot_rows, slot_rows), slot_rows)])
            live = blocks(lambda s: position < lengths[s * TOKENS : s * TOKENS + 1])
            keys = jnp.concatenate([skbuf[s] for s in slots], axis=1)
            held["scores"] = jnp.where(live, dot_t(apart(q).astype(bf16), keys) * scale, NEG_BIG)

        def weigh():
            scores = held["scores"]
            high = jnp.max(scores, axis=1, keepdims=True)
            p = jnp.exp2(scores - high)
            held["sum"] = jnp.sum(p, axis=1, keepdims=True)
            held["high"], held["p"] = high, p.astype(bf16)

        def mix():
            values = jnp.concatenate([svbuf[s] for s in slots], axis=1)
            wide = dot(held["p"], values)
            level = held["high"] + jnp.log(held["sum"]) * LOG2E
            for n, s in enumerate(slots):
                at = slice(n * slot_rows, (n + 1) * slot_rows)
                mixed = wide[at, n * HD : (n + 1) * HD]
                oraw[s] = mixed / held["sum"][at]
                lraw[s] = jnp.broadcast_to(level[at], mixed.shape)

        return [score, weigh, mix]

    def first_top():
        for r in range(0, rows, ROWBLK):
            high = jnp.max(dot_t(kbuf[0:TILE], qrow[r : r + ROWBLK]), axis=0, keepdims=True) * scale
            top[:, r : r + ROWBLK] = jnp.broadcast_to(high, (8, ROWBLK))

    def start_next(i):
        for copy in prefix_copies(i + 1):
            copy.start()
        for n in range(per_step):
            for copy in suffix_copies(i * per_step + n):
                copy.start()

    def wait_suffix(i):
        for n in range(per_step):
            for copy in suffix_copies(i * per_step + n):
                copy.wait()

    def prefix_chunk(i):
        vturn[...] = jnp.transpose(vbuf[pl.ds(pl.multiple_of(i * CHUNK, CHUNK), CHUNK)])
        blocks = [(r, t) for r in range(0, rows, ROWBLK) for t in range(0, CHUNK, KEYBLK)]

        def score(block):
            r, t = block
            keys = pl.ds(pl.multiple_of(i * CHUNK + t, KEYBLK), KEYBLK)
            return dot_t(kbuf[keys], qrow[r : r + ROWBLK])

        ready = score(blocks[0])
        mix = weight_sum = None
        for n, (r, t) in enumerate(blocks):
            scores = ready
            if n + 1 < len(blocks):
                ready = score(blocks[n + 1])
            p = jnp.exp2(scores * scale - top[0:1, r : r + ROWBLK])
            part = dot(vturn[:, t : t + KEYBLK], p.astype(bf16))
            part_sum = jnp.sum(p.reshape(KEYBLK // 8, 8, ROWBLK), axis=0)
            mix = part if t == 0 else mix + part
            weight_sum = part_sum if t == 0 else weight_sum + part_sum
            if t + KEYBLK == CHUNK:
                acc[:, r : r + ROWBLK] += mix
                total[:, r : r + ROWBLK] += weight_sum

    def step(i, unused):
        keys_copy, values_copy = prefix_copies(i)
        keys_copy.wait()
        pl.when(i + 1 < chunks)(lambda: start_next(i))
        pl.when(i == 0)(first_top)
        values_copy.wait()
        prefix_chunk(i)
        return 0

    lax.fori_loop(0, chunks, step, 0)
    summed = jnp.sum(total[...], axis=0, keepdims=True)
    total[...] = jnp.broadcast_to(summed, total.shape)

    @pl.when(jnp.logical_not(jnp.max(summed) < SAFE_SUM))
    def _():
        def safe_rows(j, unused):
            at = pl.ds(pl.multiple_of(j * ROWBLK, ROWBLK), ROWBLK)
            q = qrow[at]

            def safe_keys(i, carried):
                high, summed, mixed = carried
                keys = pl.ds(pl.multiple_of(i * TILE, TILE), TILE)
                s = dot_t(kbuf[keys], q) * scale
                new = jnp.maximum(high, jnp.max(s, axis=0, keepdims=True))
                p = jnp.exp2(s - new)
                decay = jnp.exp2(high - new)
                summed = summed * decay + jnp.sum(p, axis=0, keepdims=True)
                return new, summed, mixed * decay + dot(jnp.transpose(vbuf[keys]), p.astype(bf16))

            zero = jnp.zeros((1, ROWBLK), f32)
            high, summed, mixed = lax.fori_loop(
                0, chunks * CHUNK // TILE, safe_keys, (zero + NEG_BIG, zero, jnp.zeros((HD, ROWBLK), f32))
            )
            top[:, at] = jnp.broadcast_to(high, (8, ROWBLK))
            total[:, at] = jnp.broadcast_to(summed, (8, ROWBLK))
            acc[:, at] = mixed
            return 0

        lax.fori_loop(0, rows // ROWBLK, safe_rows, 0)

    for i in range(chunks - 1):
        wait_suffix(i)
    staged = [suffix_stages([i * per_step + n for n in range(per_step)]) for i in range(chunks - 1)]
    for m in range(3):
        for stages in staged:
            stages[m]()
    oslot[...] = jnp.zeros_like(oslot)
    lslot[...] = jnp.zeros_like(lslot)
    for s in range(slot_count):
        for g in range(groups):
            put_rows = slice(s * TOKENS, (s + 1) * TOKENS)
            lanes = slice(g * HD, (g + 1) * HD)
            oslot[put_rows, lanes] = oraw[s, g * TOKENS : (g + 1) * TOKENS]
            lslot[put_rows, lanes] = lraw[s, g * TOKENS : (g + 1) * TOKENS]
    same_row = lax.broadcasted_iota(jnp.int32, (req_rows, req_rows), 0)
    same_col = lax.broadcasted_iota(jnp.int32, (req_rows, req_rows), 1)
    put_f = dot_t(jnp.where(same_row == same_col, 1.0, 0.0).astype(bf16), pick)
    put = put_f.astype(bf16)
    suffix_mix = sum(dot(put, piece) for piece in pieces(oslot[...]))
    suffix_level = sum(dot(put, piece) for piece in pieces(lslot[...]))
    has_suffix = jnp.sum(put_f, axis=1, keepdims=True) > 0.5
    lane = lax.broadcasted_iota(jnp.int32, (req_rows, HD), 1)
    levels = jnp.zeros((req_rows, HD), f32)
    for g in range(groups):
        at = slice(g * req_rows, (g + 1) * req_rows)
        lanes = slice(g * HD, (g + 1) * HD)
        level = top[0:1, at] + jnp.log(total[0:1, at]) * LOG2E
        level = jnp.transpose(jnp.broadcast_to(level, (HD, req_rows)))
        prefix_mix = jnp.transpose(acc[:, at] / total[0:1, at])
        other = jnp.where(has_suffix, suffix_level[:, lanes], NEG_BIG)
        high = jnp.maximum(level, other)
        mine = jnp.exp2(level - high)
        theirs = jnp.exp2(other - high)
        summed = mine + theirs
        mixed = (prefix_mix * mine + suffix_mix[:, lanes] * theirs) / summed
        out_ref[:, lanes] = mixed.astype(bf16)
        level = high + jnp.log(summed) * LOG2E
        for j, piece in enumerate(pieces(level)):
            levels = jnp.where(lane == j * groups + g, piece.astype(f32), levels)
    out_ref[:, groups * HD :] = levels.astype(bf16)


def attend(table, home, gathered, prefix_k, prefix_v, suffix_k, suffix_v):
    all_rows = gathered.shape[0]
    width = gathered.shape[1]
    groups = width // HD
    rows = all_rows * groups
    slot_count = suffix_k.shape[0]
    slot_rows = groups * TOKENS
    chunks = prefix_k.shape[0] // CHUNK
    vmem = pl.BlockSpec(memory_space=pltpu.VMEM)
    hbm = pl.BlockSpec(memory_space=pl.ANY)
    return pl.pallas_call(
        functools.partial(attend_kernel, HD**-0.5 * LOG2E),
        in_specs=[vmem, vmem, vmem, hbm, hbm, hbm, hbm],
        out_specs=[vmem] * 2,
        out_shape=[
            pltpu.VMEM((all_rows, width + HD), bf16),
            pltpu.VMEM((home.shape[0], 2 * width), f32),
        ],
        scratch_shapes=[
            pltpu.VMEM(prefix_k.shape, bf16),
            pltpu.VMEM(prefix_v.shape, bf16),
            pltpu.VMEM((HD, CHUNK), bf16),
            pltpu.VMEM(suffix_k.shape, bf16),
            pltpu.VMEM(suffix_v.shape, bf16),
            pltpu.VMEM((rows, HD), bf16),
            pltpu.VMEM((8, rows), f32),
            pltpu.VMEM((HD, rows), f32),
            pltpu.VMEM((8, rows), f32),
            pltpu.VMEM((slot_count * slot_rows, HD), f32),
            pltpu.VMEM((slot_count, slot_rows, HD), f32),
            pltpu.VMEM((slot_count, slot_rows, HD), f32),
            pltpu.VMEM((PAD, width), f32),
            pltpu.VMEM((PAD, width), f32),
            pltpu.SemaphoreType.DMA((chunks,)),
            pltpu.SemaphoreType.DMA((chunks,)),
            pltpu.SemaphoreType.DMA((2, slot_count)),
        ],
        compiler_params=pltpu.CompilerParams(vmem_limit_bytes=56 * 1024 * 1024),
        name="attend",
    )(
        near(table),
        near(home),
        near(gathered),
        prefix_k,
        prefix_v,
        suffix_k,
        suffix_v,
    )


def merge_kernel(sources, copies, part_ref, fresh_ref, home_ref, out_ref):
    rows = part_ref.shape[0]
    home_rows = rows // sources
    groups = (part_ref.shape[1] - HD) // HD
    levels = part_ref[:, groups * HD :].astype(f32)
    lane = lax.broadcasted_iota(jnp.int32, (rows, HD), 1)
    value = home_ref[:, (groups + 1) * HD :]
    first_value = previous_row(value)
    for g in range(groups):
        mine = (lane % groups == g) & (lane < 3 * groups)
        level = lane_sum(jnp.where(mine, levels, 0.0)).reshape(sources, home_rows, HD)
        own = fresh_ref[:, g * HD : (g + 1) * HD]
        first = fresh_ref[:, (groups + g) * HD : (groups + g + 1) * HD]
        high = jnp.maximum(jnp.max(level, axis=0), jnp.maximum(own, first))
        weight = jnp.exp2(level - high[None])
        own = jnp.exp2(own - high)
        first = jnp.exp2(first - high)
        part = part_ref[:, g * HD : (g + 1) * HD].astype(f32).reshape(sources, home_rows, HD)
        mixed = jnp.sum(part * weight, axis=0) + own * value + first * first_value
        mixed = mixed / (jnp.sum(weight, axis=0) + own + first)
        out_ref[:, g * HD : (g + 1) * HD] = jnp.concatenate([mixed] * copies, axis=0).astype(bf16)


def on_device(queries, prefix_k, prefix_v, suffix_k, suffix_v, new_k, new_v, suffix_len, owner_of):
    req_local, tokens, width = queries.shape
    groups = width // HD
    ctx_count = lax.axis_size("ctx")
    head_count = lax.axis_size("head")
    home_rows = req_local * tokens
    all_rows = ctx_count * home_rows
    rows = all_rows * groups
    vmem = pl.BlockSpec(memory_space=pltpu.VMEM)

    sent, home, table = pl.pallas_call(
        functools.partial(spread_kernel, ctx_count),
        in_specs=[vmem] * 5,
        out_specs=[vmem] * 3,
        out_shape=[
            pltpu.VMEM((all_rows, width), bf16),
            pltpu.VMEM((home_rows, width + 2 * HD), f32),
            pltpu.VMEM((2, owner_of.shape[0]), jnp.int32),
        ],
        name="spread",
    )(queries, new_k, new_v, owner_of.reshape(1, -1), suffix_len.reshape(1, -1))
    gathered = lax.all_to_all(sent, "ctx", split_axis=0, concat_axis=0, tiled=True)

    parts, fresh = attend(table, home, gathered, prefix_k, prefix_v, suffix_k, suffix_v)
    arrived = lax.all_to_all(parts, "ctx", split_axis=0, concat_axis=0, tiled=True)

    finished = pl.pallas_call(
        functools.partial(merge_kernel, ctx_count, head_count),
        in_specs=[vmem] * 3,
        out_specs=vmem,
        out_shape=pltpu.VMEM((head_count * home_rows, width), bf16),
        name="merge",
    )(near(arrived), near(fresh), near(home))
    heads = lax.all_to_all(finished, "head", split_axis=0, concat_axis=0, tiled=True)
    heads = heads.reshape(head_count, home_rows, width).transpose(1, 0, 2)
    return heads.reshape(req_local, tokens, head_count * width)


def solution(mesh):
    placed = (
        P("ctx", None, "head"),
        P("ctx", "head"),
        P("ctx", "head"),
        P("ctx", None, "head"),
        P("ctx", None, "head"),
        P("ctx", None, "head"),
        P("ctx", None, "head"),
        P(),
        P(),
    )
    return jax.shard_map(
        on_device, mesh=mesh, in_specs=placed, out_specs=P("ctx", None, None), check_vma=False
    )
```

```python
import functools

import jax
import jax.numpy as jnp
from jax import lax
from jax.experimental import pallas as pl
from jax.experimental.pallas import tpu as pltpu
from jax.sharding import PartitionSpec as P

H = 64
KV = 8
HD = 128
LOG2E = 1.4426950408889634
NEG_BIG = -1e30
SAFE_SUM = 2.0**60

TOKENS = 2
PAD = 16
CHUNK = 4096
TILE = 256
ROWBLK = 256
KEYBLK = 1024
SUFFIX_ORDER = ((0, 0), (1, 0), (0, 1), (2, 0), (1, 1), (0, 2), (2, 1), (1, 2), (2, 2))

f32 = jnp.float32
bf16 = jnp.bfloat16


def dot(a, b):
    return lax.dot_general(a, b, (((1,), (0,)), ((), ())), preferred_element_type=f32)


def dot_t(a, b):
    return lax.dot_general(a, b, (((1,), (1,)), ((), ())), preferred_element_type=f32)


def near(x):
    return pltpu.with_memory_space_constraint(x, pltpu.VMEM)


def lane_sum(x):
    return jnp.broadcast_to(jnp.sum(x, axis=1, keepdims=True), x.shape)


def pieces(x):
    first = x.astype(bf16)
    rest = x - first.astype(f32)
    second = rest.astype(bf16)
    third = (rest - second.astype(f32)).astype(bf16)
    return first, second, third


def previous_row(x):
    return jnp.concatenate([x[-1:], x[:-1]], axis=0)


def spread_kernel(copies, q_ref, k_ref, v_ref, owner_ref, length_ref, out_ref, home_ref, table_ref):
    rows = q_ref.shape[0] * q_ref.shape[1]
    width = q_ref.shape[2]
    block = q_ref[...].astype(f32).reshape(rows, width)
    out_ref[...] = jnp.concatenate([block] * copies, axis=0).astype(bf16)
    home_ref[:, :width] = block
    home_ref[:, width : width + HD] = k_ref[...].astype(f32).reshape(rows, HD)
    home_ref[:, width + HD :] = v_ref[...].astype(f32).reshape(rows, HD)
    table_ref[0:1] = owner_ref[...]
    table_ref[1:2] = length_ref[...]


def attend_kernel(
    scale, table_ref, home_ref, q_ref, pk_ref, pv_ref, sk_ref, sv_ref, out_ref, fresh_ref,
    kbuf, vbuf, vturn, skbuf, svbuf, qrow, top, acc, total, qslot, oslot, lslot, ksem, vsem, ssem,
):
    req_rows = q_ref.shape[0]
    groups = q_ref.shape[1] // HD
    rows = req_rows * groups
    slot_count, span = sk_ref.shape[0], sk_ref.shape[1]
    slot_rows = groups * TOKENS
    chunks = pk_ref.shape[0] // CHUNK
    per_step = slot_count // (chunks - 1)

    def prefix_copies(i):
        at = pl.ds(i * CHUNK, CHUNK)
        return (
            pltpu.make_async_copy(pk_ref.at[at], kbuf.at[at], ksem.at[i]),
            pltpu.make_async_copy(pv_ref.at[at], vbuf.at[at], vsem.at[i]),
        )

    def suffix_copies(i, n):
        s = i * per_step + n
        lanes = pl.ds(n * HD, HD)
        return (
            pltpu.make_async_copy(sk_ref.at[s], skbuf.at[i, :, lanes], ssem.at[0, s]),
            pltpu.make_async_copy(sv_ref.at[s], svbuf.at[i, :, lanes], ssem.at[1, s]),
        )

    for copy in prefix_copies(0):
        copy.start()

    for g in range(groups):
        qrow[g * req_rows : (g + 1) * req_rows] = q_ref[:, g * HD : (g + 1) * HD]
    acc[...] = jnp.zeros_like(acc)
    total[...] = jnp.zeros_like(total)

    key = home_ref[:, groups * HD : (groups + 1) * HD]
    second = lax.broadcasted_iota(jnp.int32, key.shape, 0) % TOKENS == 1
    for g in range(groups):
        q = home_ref[:, g * HD : (g + 1) * HD]
        fresh_ref[:, g * HD : (g + 1) * HD] = lane_sum(q * key) * scale
        first = lane_sum(q * previous_row(key)) * scale
        fresh_ref[:, (groups + g) * HD : (groups + g + 1) * HD] = jnp.where(second, first, NEG_BIG)

    requests = table_ref.shape[1]
    base = lax.axis_index("ctx") * slot_count
    slot_of = lax.broadcasted_iota(jnp.int32, (PAD, requests), 0) // TOKENS
    owned = (table_ref[0:1] == base + slot_of) & (slot_of < slot_count)
    lengths = jnp.sum(jnp.where(owned, table_ref[1:2], 0), axis=1, keepdims=True)
    spread_row = lax.broadcasted_iota(jnp.int32, (requests, req_rows), 0)
    spread_col = lax.broadcasted_iota(jnp.int32, (requests, req_rows), 1)
    spread = jnp.where(spread_col // TOKENS == spread_row, 1.0, 0.0).astype(bf16)
    pick_row = lax.broadcasted_iota(jnp.int32, (PAD, req_rows), 0)
    pick_col = lax.broadcasted_iota(jnp.int32, (PAD, req_rows), 1)
    pick = dot(jnp.where(owned, 1.0, 0.0).astype(bf16), spread)
    pick = jnp.where(pick_row % TOKENS == pick_col % TOKENS, pick, 0.0).astype(bf16)
    picked = dot(pick, q_ref[...])
    for s in range(slot_count):
        for g in range(groups):
            qslot[s * slot_rows + g * TOKENS : s * slot_rows + (g + 1) * TOKENS] = picked[
                s * TOKENS : (s + 1) * TOKENS, g * HD : (g + 1) * HD
            ]
    position = lax.broadcasted_iota(jnp.int32, (slot_rows, span), 1)

    def suffix_stages(slots):
        held = {}
        count = len(slots)

        def blocks(make):
            return jnp.concatenate([make(s) for s in slots], axis=0)

        def apart(x):
            zero = jnp.zeros((slot_rows, HD), x.dtype)
            own = [x[n * slot_rows : (n + 1) * slot_rows] for n in range(count)]
            return jnp.concatenate(
                [jnp.concatenate([own[n] if m == n else zero for m in range(count)], axis=1) for n in range(count)],
                axis=0,
            )

        def score():
            q = blocks(lambda s: qslot[pl.ds(pl.multiple_of(s * slot_rows, slot_rows), slot_rows)])
            live = blocks(lambda s: position < lengths[s * TOKENS : s * TOKENS + 1])
            keys = skbuf[slots[0] // per_step]
            held["scores"] = jnp.where(live, jnp.transpose(dot_t(keys, apart(q).astype(bf16))) * scale, NEG_BIG)

        def weigh():
            scores = held["scores"]
            high = jnp.max(scores, axis=1, keepdims=True)
            p = jnp.exp2(scores - high)
            held["sum"] = jnp.sum(p, axis=1, keepdims=True)
            held["high"], held["p"] = high, p.astype(bf16)

        def mix():
            values = svbuf[slots[0] // per_step]
            wide = dot(held["p"], values)
            level = held["high"] + jnp.log(held["sum"]) * LOG2E
            for n, s in enumerate(slots):
                at = slice(n * slot_rows, (n + 1) * slot_rows)
                mixed = wide[at, n * HD : (n + 1) * HD]
                mixed = mixed * (1.0 / held["sum"][at])
                wide_level = jnp.broadcast_to(level[at], mixed.shape)
                for g in range(groups):
                    put_rows = slice(s * TOKENS, (s + 1) * TOKENS)
                    lanes = slice(g * HD, (g + 1) * HD)
                    oslot[put_rows, lanes] = mixed[g * TOKENS : (g + 1) * TOKENS]
                    lslot[put_rows, lanes] = wide_level[g * TOKENS : (g + 1) * TOKENS]

        return [score, weigh, mix]

    def first_top():
        for r in range(0, rows, ROWBLK):
            high = jnp.max(dot_t(kbuf[0:TILE], qrow[r : r + ROWBLK]), axis=0, keepdims=True) * scale
            top[:, r : r + ROWBLK] = jnp.broadcast_to(high, (8, ROWBLK))

    def start_next(i):
        for copy in prefix_copies(i + 1):
            copy.start()
        for n in range(per_step):
            for copy in suffix_copies(i, n):
                copy.start()

    def wait_suffix(i):
        for n in range(per_step):
            for copy in suffix_copies(i, n):
                copy.wait()

    def prefix_chunk(i):
        vturn[...] = jnp.transpose(vbuf[pl.ds(pl.multiple_of(i * CHUNK, CHUNK), CHUNK)])
        blocks = [(r, t) for r in range(0, rows, ROWBLK) for t in range(0, CHUNK, KEYBLK)]

        def score(block):
            r, t = block
            keys = pl.ds(pl.multiple_of(i * CHUNK + t, KEYBLK), KEYBLK)
            return dot_t(kbuf[keys], qrow[r : r + ROWBLK])

        ready = score(blocks[0])
        mix = weight_sum = None
        for n, (r, t) in enumerate(blocks):
            scores = ready
            if n + 1 < len(blocks):
                ready = score(blocks[n + 1])
            p = jnp.exp2(scores * scale - top[0:1, r : r + ROWBLK])
            part = dot(vturn[:, t : t + KEYBLK], p.astype(bf16))
            part_sum = jnp.sum(p.reshape(KEYBLK // 8, 8, ROWBLK), axis=0)
            mix = part if t == 0 else mix + part
            weight_sum = part_sum if t == 0 else weight_sum + part_sum
            if t + KEYBLK == CHUNK:
                acc[:, r : r + ROWBLK] += mix
                total[:, r : r + ROWBLK] += weight_sum

    def step(i, unused):
        keys_copy, values_copy = prefix_copies(i)
        keys_copy.wait()
        pl.when(i + 1 < chunks)(lambda: start_next(i))
        pl.when(i == 0)(first_top)
        values_copy.wait()
        prefix_chunk(i)
        return 0

    lax.fori_loop(0, chunks, step, 0)
    summed = jnp.sum(total[...], axis=0, keepdims=True)
    total[...] = jnp.broadcast_to(summed, total.shape)

    @pl.when(jnp.logical_not(jnp.max(summed) < SAFE_SUM))
    def _():
        def safe_rows(j, unused):
            at = pl.ds(pl.multiple_of(j * ROWBLK, ROWBLK), ROWBLK)
            q = qrow[at]

            def safe_keys(i, carried):
                high, summed, mixed = carried
                keys = pl.ds(pl.multiple_of(i * TILE, TILE), TILE)
                s = dot_t(kbuf[keys], q) * scale
                new = jnp.maximum(high, jnp.max(s, axis=0, keepdims=True))
                p = jnp.exp2(s - new)
                decay = jnp.exp2(high - new)
                summed = summed * decay + jnp.sum(p, axis=0, keepdims=True)
                return new, summed, mixed * decay + dot(jnp.transpose(vbuf[keys]), p.astype(bf16))

            zero = jnp.zeros((1, ROWBLK), f32)
            high, summed, mixed = lax.fori_loop(
                0, chunks * CHUNK // TILE, safe_keys, (zero + NEG_BIG, zero, jnp.zeros((HD, ROWBLK), f32))
            )
            top[:, at] = jnp.broadcast_to(high, (8, ROWBLK))
            total[:, at] = jnp.broadcast_to(summed, (8, ROWBLK))
            acc[:, at] = mixed
            return 0

        lax.fori_loop(0, rows // ROWBLK, safe_rows, 0)

    for i in range(chunks - 1):
        wait_suffix(i)
    staged = [suffix_stages([i * per_step + n for n in range(per_step)]) for i in range(chunks - 1)]
    oslot[...] = jnp.zeros_like(oslot)
    lslot[...] = jnp.zeros_like(lslot)
    for pair, m in SUFFIX_ORDER:
        staged[pair][m]()
    same_row = lax.broadcasted_iota(jnp.int32, (req_rows, req_rows), 0)
    same_col = lax.broadcasted_iota(jnp.int32, (req_rows, req_rows), 1)
    put_f = dot_t(jnp.where(same_row == same_col, 1.0, 0.0).astype(bf16), pick)
    put = jnp.concatenate([put_f] * 3, axis=1).astype(bf16)
    suffix_mix = dot(put, jnp.concatenate(pieces(oslot[...]), axis=0))
    suffix_level = dot(put, jnp.concatenate(pieces(lslot[...]), axis=0))
    has_suffix = jnp.sum(put_f, axis=1, keepdims=True) > 0.5
    lane = lax.broadcasted_iota(jnp.int32, (req_rows, HD), 1)
    levels = jnp.zeros((req_rows, HD), f32)
    for g in range(groups):
        at = slice(g * req_rows, (g + 1) * req_rows)
        lanes = slice(g * HD, (g + 1) * HD)
        level = top[0:1, at] + jnp.log(total[0:1, at]) * LOG2E
        level = jnp.transpose(jnp.broadcast_to(level, (HD, req_rows)))
        prefix_mix = jnp.transpose(acc[:, at] * (1.0 / total[0:1, at]))
        other = jnp.where(has_suffix, suffix_level[:, lanes], NEG_BIG)
        high = jnp.maximum(level, other)
        mine = jnp.exp2(level - high)
        theirs = jnp.exp2(other - high)
        summed = mine + theirs
        mixed = (prefix_mix * mine + suffix_mix[:, lanes] * theirs) * (1.0 / summed)
        out_ref[:, lanes] = mixed.astype(bf16)
        level = high + jnp.log(summed) * LOG2E
        for j, piece in enumerate(pieces(level)):
            levels = jnp.where(lane == j * groups + g, piece.astype(f32), levels)
    out_ref[:, groups * HD :] = levels.astype(bf16)


def attend(table, home, gathered, prefix_k, prefix_v, suffix_k, suffix_v):
    all_rows = gathered.shape[0]
    width = gathered.shape[1]
    groups = width // HD
    rows = all_rows * groups
    slot_count = suffix_k.shape[0]
    slot_rows = groups * TOKENS
    chunks = prefix_k.shape[0] // CHUNK
    per_step = slot_count // (chunks - 1)
    paired = (slot_count // per_step, suffix_k.shape[1], per_step * HD)
    vmem = pl.BlockSpec(memory_space=pltpu.VMEM)
    hbm = pl.BlockSpec(memory_space=pl.ANY)
    return pl.pallas_call(
        functools.partial(attend_kernel, HD**-0.5 * LOG2E),
        in_specs=[vmem, vmem, vmem, hbm, hbm, hbm, hbm],
        out_specs=[vmem] * 2,
        out_shape=[
            pltpu.VMEM((all_rows, width + HD), bf16),
            pltpu.VMEM((home.shape[0], 2 * width), f32),
        ],
        scratch_shapes=[
            pltpu.VMEM(prefix_k.shape, bf16),
            pltpu.VMEM(prefix_v.shape, bf16),
            pltpu.VMEM((HD, CHUNK), bf16),
            pltpu.VMEM(paired, bf16),
            pltpu.VMEM(paired, bf16),
            pltpu.VMEM((rows, HD), bf16),
            pltpu.VMEM((8, rows), f32),
            pltpu.VMEM((HD, rows), f32),
            pltpu.VMEM((8, rows), f32),
            pltpu.VMEM((slot_count * slot_rows, HD), f32),
            pltpu.VMEM((PAD, width), f32),
            pltpu.VMEM((PAD, width), f32),
            pltpu.SemaphoreType.DMA((chunks,)),
            pltpu.SemaphoreType.DMA((chunks,)),
            pltpu.SemaphoreType.DMA((2, slot_count)),
        ],
        compiler_params=pltpu.CompilerParams(vmem_limit_bytes=56 * 1024 * 1024),
        name="attend",
    )(
        near(table),
        near(home),
        near(gathered),
        prefix_k,
        prefix_v,
        suffix_k,
        suffix_v,
    )


def merge_kernel(sources, copies, part_ref, fresh_ref, home_ref, out_ref):
    rows = part_ref.shape[0]
    home_rows = rows // sources
    groups = (part_ref.shape[1] - HD) // HD
    levels = part_ref[:, groups * HD :].astype(f32)
    lane = lax.broadcasted_iota(jnp.int32, (rows, HD), 1)
    value = home_ref[:, (groups + 1) * HD :]
    first_value = previous_row(value)
    for g in range(groups):
        mine = (lane % groups == g) & (lane < 3 * groups)
        level = lane_sum(jnp.where(mine, levels, 0.0)).reshape(sources, home_rows, HD)
        own = fresh_ref[:, g * HD : (g + 1) * HD]
        first = fresh_ref[:, (groups + g) * HD : (groups + g + 1) * HD]
        high = jnp.maximum(jnp.max(level, axis=0), jnp.maximum(own, first))
        weight = jnp.exp2(level - high[None])
        own = jnp.exp2(own - high)
        first = jnp.exp2(first - high)
        part = part_ref[:, g * HD : (g + 1) * HD].astype(f32).reshape(sources, home_rows, HD)
        mixed = jnp.sum(part * weight, axis=0) + own * value + first * first_value
        mixed = mixed / (jnp.sum(weight, axis=0) + own + first)
        out_ref[:, g * HD : (g + 1) * HD] = jnp.concatenate([mixed] * copies, axis=0).astype(bf16)


def on_device(queries, prefix_k, prefix_v, suffix_k, suffix_v, new_k, new_v, suffix_len, owner_of):
    req_local, tokens, width = queries.shape
    groups = width // HD
    ctx_count = lax.axis_size("ctx")
    head_count = lax.axis_size("head")
    home_rows = req_local * tokens
    all_rows = ctx_count * home_rows
    rows = all_rows * groups
    vmem = pl.BlockSpec(memory_space=pltpu.VMEM)

    sent, home, table = pl.pallas_call(
        functools.partial(spread_kernel, ctx_count),
        in_specs=[vmem] * 5,
        out_specs=[vmem] * 3,
        out_shape=[
            pltpu.VMEM((all_rows, width), bf16),
            pltpu.VMEM((home_rows, width + 2 * HD), f32),
            pltpu.VMEM((2, owner_of.shape[0]), jnp.int32),
        ],
        name="spread",
    )(queries, new_k, new_v, owner_of.reshape(1, -1), suffix_len.reshape(1, -1))
    gathered = lax.all_to_all(sent, "ctx", split_axis=0, concat_axis=0, tiled=True)

    parts, fresh = attend(table, home, gathered, prefix_k, prefix_v, suffix_k, suffix_v)
    arrived = lax.all_to_all(parts, "ctx", split_axis=0, concat_axis=0, tiled=True)

    finished = pl.pallas_call(
        functools.partial(merge_kernel, ctx_count, head_count),
        in_specs=[vmem] * 3,
        out_specs=vmem,
        out_shape=pltpu.VMEM((head_count * home_rows, width), bf16),
        name="merge",
    )(near(arrived), near(fresh), near(home))
    heads = lax.all_to_all(finished, "head", split_axis=0, concat_axis=0, tiled=True)
    heads = heads.reshape(head_count, home_rows, width).transpose(1, 0, 2)
    return heads.reshape(req_local, tokens, head_count * width)


def solution(mesh):
    placed = (
        P("ctx", None, "head"),
        P("ctx", "head"),
        P("ctx", "head"),
        P("ctx", None, "head"),
        P("ctx", None, "head"),
        P("ctx", None, "head"),
        P("ctx", None, "head"),
        P(),
        P(),
    )
    return jax.shard_map(
        on_device, mesh=mesh, in_specs=placed, out_specs=P("ctx", None, None), check_vma=False
    )
```

```python
import functools

import jax
import jax.numpy as jnp
from jax import lax
from jax.experimental import pallas as pl
from jax.experimental.pallas import tpu as pltpu
from jax.sharding import PartitionSpec as P

H = 64
KV = 8
HD = 128
LOG2E = 1.4426950408889634
NEG_BIG = -1e30
SAFE_SUM = 2.0**60

TOKENS = 2
PAD = 16
CHUNK = 4096
TILE = 256
ROWBLK = 256
KEYBLK = 1024
SUFFIX_ORDER = ((0, 0), (1, 0), (0, 1), (2, 0), (1, 1), (0, 2), (2, 1), (1, 2), (2, 2))

f32 = jnp.float32
bf16 = jnp.bfloat16


def dot(a, b):
    return lax.dot_general(a, b, (((1,), (0,)), ((), ())), preferred_element_type=f32)


def dot_t(a, b):
    return lax.dot_general(a, b, (((1,), (1,)), ((), ())), preferred_element_type=f32)


def near(x):
    return pltpu.with_memory_space_constraint(x, pltpu.VMEM)


def lane_sum(x):
    return jnp.broadcast_to(jnp.sum(x, axis=1, keepdims=True), x.shape)


def pieces(x):
    first = x.astype(bf16)
    rest = x - first.astype(f32)
    second = rest.astype(bf16)
    third = (rest - second.astype(f32)).astype(bf16)
    return first, second, third


def previous_row(x):
    return jnp.concatenate([x[-1:], x[:-1]], axis=0)


def spread_kernel(copies, q_ref, k_ref, v_ref, owner_ref, length_ref, out_ref, home_ref, table_ref):
    rows = q_ref.shape[0] * q_ref.shape[1]
    width = q_ref.shape[2]
    block = q_ref[...].astype(f32).reshape(rows, width)
    out_ref[...] = jnp.concatenate([block] * copies, axis=0).astype(bf16)
    home_ref[:, :width] = block
    home_ref[:, width : width + HD] = k_ref[...].astype(f32).reshape(rows, HD)
    home_ref[:, width + HD :] = v_ref[...].astype(f32).reshape(rows, HD)
    table_ref[0:1] = owner_ref[...]
    table_ref[1:2] = length_ref[...]


def attend_kernel(
    scale, table_ref, home_ref, q_ref, pk_ref, pv_ref, sk_ref, sv_ref, out_ref, fresh_ref,
    kfirst, kbuf, vbuf, vturn, skbuf, svbuf, qrow, top, acc, total, qslot, oslot, lslot, fsem, ksem, vsem, ssem,
):
    req_rows = q_ref.shape[0]
    groups = q_ref.shape[1] // HD
    rows = req_rows * groups
    slot_count, span = sk_ref.shape[0], sk_ref.shape[1]
    slot_rows = groups * TOKENS
    chunks = pk_ref.shape[0] // CHUNK
    per_step = slot_count // (chunks - 1)

    def prefix_copies(i):
        at = pl.ds(i * CHUNK, CHUNK)
        return (
            pltpu.make_async_copy(pk_ref.at[at], kbuf.at[at], ksem.at[i]),
            pltpu.make_async_copy(pv_ref.at[at], vbuf.at[at], vsem.at[i]),
        )

    def suffix_copies(i, n):
        s = i * per_step + n
        lanes = pl.ds(n * HD, HD)
        return (
            pltpu.make_async_copy(sk_ref.at[s], skbuf.at[i, :, lanes], ssem.at[0, s]),
            pltpu.make_async_copy(sv_ref.at[s], svbuf.at[i, :, lanes], ssem.at[1, s]),
        )

    first_keys = pltpu.make_async_copy(pk_ref.at[pl.ds(0, TILE)], kfirst, fsem)
    first_keys.start()
    for copy in prefix_copies(0):
        copy.start()

    for g in range(groups):
        qrow[g * req_rows : (g + 1) * req_rows] = q_ref[:, g * HD : (g + 1) * HD]
    acc[...] = jnp.zeros_like(acc)
    total[...] = jnp.zeros_like(total)

    key = home_ref[:, groups * HD : (groups + 1) * HD]
    second = lax.broadcasted_iota(jnp.int32, key.shape, 0) % TOKENS == 1
    for g in range(groups):
        q = home_ref[:, g * HD : (g + 1) * HD]
        fresh_ref[:, g * HD : (g + 1) * HD] = lane_sum(q * key) * scale
        first = lane_sum(q * previous_row(key)) * scale
        fresh_ref[:, (groups + g) * HD : (groups + g + 1) * HD] = jnp.where(second, first, NEG_BIG)

    requests = table_ref.shape[1]
    base = lax.axis_index("ctx") * slot_count
    slot_of = lax.broadcasted_iota(jnp.int32, (PAD, requests), 0) // TOKENS
    owned = (table_ref[0:1] == base + slot_of) & (slot_of < slot_count)
    lengths = jnp.sum(jnp.where(owned, table_ref[1:2], 0), axis=1, keepdims=True)
    spread_row = lax.broadcasted_iota(jnp.int32, (requests, req_rows), 0)
    spread_col = lax.broadcasted_iota(jnp.int32, (requests, req_rows), 1)
    spread = jnp.where(spread_col // TOKENS == spread_row, 1.0, 0.0).astype(bf16)
    pick_row = lax.broadcasted_iota(jnp.int32, (PAD, req_rows), 0)
    pick_col = lax.broadcasted_iota(jnp.int32, (PAD, req_rows), 1)
    pick = dot(jnp.where(owned, 1.0, 0.0).astype(bf16), spread)
    pick = jnp.where(pick_row % TOKENS == pick_col % TOKENS, pick, 0.0).astype(bf16)
    picked = dot(pick, q_ref[...])
    for s in range(slot_count):
        for g in range(groups):
            qslot[s * slot_rows + g * TOKENS : s * slot_rows + (g + 1) * TOKENS] = picked[
                s * TOKENS : (s + 1) * TOKENS, g * HD : (g + 1) * HD
            ]
    position = lax.broadcasted_iota(jnp.int32, (slot_rows, span), 1)

    def suffix_stages(slots):
        held = {}
        count = len(slots)

        def blocks(make):
            return jnp.concatenate([make(s) for s in slots], axis=0)

        def apart(x):
            zero = jnp.zeros((slot_rows, HD), x.dtype)
            own = [x[n * slot_rows : (n + 1) * slot_rows] for n in range(count)]
            return jnp.concatenate(
                [jnp.concatenate([own[n] if m == n else zero for m in range(count)], axis=1) for n in range(count)],
                axis=0,
            )

        def score():
            q = blocks(lambda s: qslot[pl.ds(pl.multiple_of(s * slot_rows, slot_rows), slot_rows)])
            live = blocks(lambda s: position < lengths[s * TOKENS : s * TOKENS + 1])
            keys = skbuf[slots[0] // per_step]
            held["scores"] = jnp.where(live, jnp.transpose(dot_t(keys, apart(q).astype(bf16))) * scale, NEG_BIG)

        def weigh():
            scores = held["scores"]
            high = jnp.max(scores, axis=1, keepdims=True)
            p = jnp.exp2(scores - high)
            held["sum"] = jnp.sum(p, axis=1, keepdims=True)
            held["high"], held["p"] = high, p.astype(bf16)

        def mix():
            values = svbuf[slots[0] // per_step]
            wide = dot(held["p"], values)
            level = held["high"] + jnp.log(held["sum"]) * LOG2E
            for n, s in enumerate(slots):
                at = slice(n * slot_rows, (n + 1) * slot_rows)
                mixed = wide[at, n * HD : (n + 1) * HD]
                mixed = mixed * (1.0 / held["sum"][at])
                wide_level = jnp.broadcast_to(level[at], mixed.shape)
                for g in range(groups):
                    put_rows = slice(s * TOKENS, (s + 1) * TOKENS)
                    lanes = slice(g * HD, (g + 1) * HD)
                    oslot[put_rows, lanes] = mixed[g * TOKENS : (g + 1) * TOKENS]
                    lslot[put_rows, lanes] = wide_level[g * TOKENS : (g + 1) * TOKENS]

        return [score, weigh, mix]

    def first_top():
        for r in range(0, rows, ROWBLK):
            high = jnp.max(dot_t(kfirst[...], qrow[r : r + ROWBLK]), axis=0, keepdims=True) * scale
            top[:, r : r + ROWBLK] = jnp.broadcast_to(high, (8, ROWBLK))

    def start_next(i):
        for copy in prefix_copies(i + 1):
            copy.start()
        for n in range(per_step):
            for copy in suffix_copies(i, n):
                copy.start()

    def wait_suffix(i):
        for n in range(per_step):
            for copy in suffix_copies(i, n):
                copy.wait()

    def prefix_chunk(i):
        vturn[...] = jnp.transpose(vbuf[pl.ds(pl.multiple_of(i * CHUNK, CHUNK), CHUNK)])
        blocks = [(r, t) for r in range(0, rows, ROWBLK) for t in range(0, CHUNK, KEYBLK)]

        def score(block):
            r, t = block
            keys = pl.ds(pl.multiple_of(i * CHUNK + t, KEYBLK), KEYBLK)
            return dot_t(kbuf[keys], qrow[r : r + ROWBLK])

        ready = score(blocks[0])
        mix = weight_sum = None
        for n, (r, t) in enumerate(blocks):
            scores = ready
            if n + 1 < len(blocks):
                ready = score(blocks[n + 1])
            p = jnp.exp2(scores * scale - top[0:1, r : r + ROWBLK])
            part = dot(vturn[:, t : t + KEYBLK], p.astype(bf16))
            part_sum = jnp.sum(p.reshape(KEYBLK // 8, 8, ROWBLK), axis=0)
            mix = part if t == 0 else mix + part
            weight_sum = part_sum if t == 0 else weight_sum + part_sum
            if t + KEYBLK == CHUNK:
                acc[:, r : r + ROWBLK] += mix
                total[:, r : r + ROWBLK] += weight_sum

    def step(i, unused):
        keys_copy, values_copy = prefix_copies(i)
        keys_copy.wait()
        pl.when(i + 1 < chunks)(lambda: start_next(i))
        values_copy.wait()
        prefix_chunk(i)
        return 0

    first_keys.wait()
    first_top()
    lax.fori_loop(0, chunks, step, 0)
    summed = jnp.sum(total[...], axis=0, keepdims=True)
    total[...] = jnp.broadcast_to(summed, total.shape)

    @pl.when(jnp.logical_not(jnp.max(summed) < SAFE_SUM))
    def _():
        def safe_rows(j, unused):
            at = pl.ds(pl.multiple_of(j * ROWBLK, ROWBLK), ROWBLK)
            q = qrow[at]

            def safe_keys(i, carried):
                high, summed, mixed = carried
                keys = pl.ds(pl.multiple_of(i * TILE, TILE), TILE)
                s = dot_t(kbuf[keys], q) * scale
                new = jnp.maximum(high, jnp.max(s, axis=0, keepdims=True))
                p = jnp.exp2(s - new)
                decay = jnp.exp2(high - new)
                summed = summed * decay + jnp.sum(p, axis=0, keepdims=True)
                return new, summed, mixed * decay + dot(jnp.transpose(vbuf[keys]), p.astype(bf16))

            zero = jnp.zeros((1, ROWBLK), f32)
            high, summed, mixed = lax.fori_loop(
                0, chunks * CHUNK // TILE, safe_keys, (zero + NEG_BIG, zero, jnp.zeros((HD, ROWBLK), f32))
            )
            top[:, at] = jnp.broadcast_to(high, (8, ROWBLK))
            total[:, at] = jnp.broadcast_to(summed, (8, ROWBLK))
            acc[:, at] = mixed
            return 0

        lax.fori_loop(0, rows // ROWBLK, safe_rows, 0)

    for i in range(chunks - 1):
        wait_suffix(i)
    staged = [suffix_stages([i * per_step + n for n in range(per_step)]) for i in range(chunks - 1)]
    oslot[...] = jnp.zeros_like(oslot)
    lslot[...] = jnp.zeros_like(lslot)
    for pair, m in SUFFIX_ORDER:
        staged[pair][m]()
    same_row = lax.broadcasted_iota(jnp.int32, (req_rows, req_rows), 0)
    same_col = lax.broadcasted_iota(jnp.int32, (req_rows, req_rows), 1)
    put_f = dot_t(jnp.where(same_row == same_col, 1.0, 0.0).astype(bf16), pick)
    put = jnp.concatenate([put_f] * 3, axis=1).astype(bf16)
    suffix_mix = dot(put, jnp.concatenate(pieces(oslot[...]), axis=0))
    suffix_level = dot(put, jnp.concatenate(pieces(lslot[...]), axis=0))
    has_suffix = jnp.sum(put_f, axis=1, keepdims=True) > 0.5
    lane = lax.broadcasted_iota(jnp.int32, (req_rows, HD), 1)
    levels = jnp.zeros((req_rows, HD), f32)
    for g in range(groups):
        at = slice(g * req_rows, (g + 1) * req_rows)
        lanes = slice(g * HD, (g + 1) * HD)
        level = top[0:1, at] + jnp.log(total[0:1, at]) * LOG2E
        level = jnp.transpose(jnp.broadcast_to(level, (HD, req_rows)))
        prefix_mix = jnp.transpose(acc[:, at] * (1.0 / total[0:1, at]))
        other = jnp.where(has_suffix, suffix_level[:, lanes], NEG_BIG)
        high = jnp.maximum(level, other)
        mine = jnp.exp2(level - high)
        theirs = jnp.exp2(other - high)
        summed = mine + theirs
        mixed = (prefix_mix * mine + suffix_mix[:, lanes] * theirs) * (1.0 / summed)
        out_ref[:, lanes] = mixed.astype(bf16)
        level = high + jnp.log(summed) * LOG2E
        for j, piece in enumerate(pieces(level)):
            levels = jnp.where(lane == j * groups + g, piece.astype(f32), levels)
    out_ref[:, groups * HD :] = levels.astype(bf16)


def attend(table, home, gathered, prefix_k, prefix_v, suffix_k, suffix_v):
    all_rows = gathered.shape[0]
    width = gathered.shape[1]
    groups = width // HD
    rows = all_rows * groups
    slot_count = suffix_k.shape[0]
    slot_rows = groups * TOKENS
    chunks = prefix_k.shape[0] // CHUNK
    per_step = slot_count // (chunks - 1)
    paired = (slot_count // per_step, suffix_k.shape[1], per_step * HD)
    vmem = pl.BlockSpec(memory_space=pltpu.VMEM)
    hbm = pl.BlockSpec(memory_space=pl.ANY)
    return pl.pallas_call(
        functools.partial(attend_kernel, HD**-0.5 * LOG2E),
        in_specs=[vmem, vmem, vmem, hbm, hbm, hbm, hbm],
        out_specs=[vmem] * 2,
        out_shape=[
            pltpu.VMEM((all_rows, width + HD), bf16),
            pltpu.VMEM((home.shape[0], 2 * width), f32),
        ],
        scratch_shapes=[
            pltpu.VMEM((TILE, HD), bf16),
            pltpu.VMEM(prefix_k.shape, bf16),
            pltpu.VMEM(prefix_v.shape, bf16),
            pltpu.VMEM((HD, CHUNK), bf16),
            pltpu.VMEM(paired, bf16),
            pltpu.VMEM(paired, bf16),
            pltpu.VMEM((rows, HD), bf16),
            pltpu.VMEM((8, rows), f32),
            pltpu.VMEM((HD, rows), f32),
            pltpu.VMEM((8, rows), f32),
            pltpu.VMEM((slot_count * slot_rows, HD), f32),
            pltpu.VMEM((PAD, width), f32),
            pltpu.VMEM((PAD, width), f32),
            pltpu.SemaphoreType.DMA,
            pltpu.SemaphoreType.DMA((chunks,)),
            pltpu.SemaphoreType.DMA((chunks,)),
            pltpu.SemaphoreType.DMA((2, slot_count)),
        ],
        compiler_params=pltpu.CompilerParams(vmem_limit_bytes=56 * 1024 * 1024),
        name="attend",
    )(
        near(table),
        near(home),
        near(gathered),
        prefix_k,
        prefix_v,
        suffix_k,
        suffix_v,
    )


def merge_kernel(sources, copies, part_ref, fresh_ref, home_ref, out_ref):
    rows = part_ref.shape[0]
    home_rows = rows // sources
    groups = (part_ref.shape[1] - HD) // HD
    levels = part_ref[:, groups * HD :].astype(f32)
    lane = lax.broadcasted_iota(jnp.int32, (rows, HD), 1)
    value = home_ref[:, (groups + 1) * HD :]
    first_value = previous_row(value)
    for g in range(groups):
        mine = (lane % groups == g) & (lane < 3 * groups)
        level = lane_sum(jnp.where(mine, levels, 0.0)).reshape(sources, home_rows, HD)
        own = fresh_ref[:, g * HD : (g + 1) * HD]
        first = fresh_ref[:, (groups + g) * HD : (groups + g + 1) * HD]
        high = jnp.maximum(jnp.max(level, axis=0), jnp.maximum(own, first))
        weight = jnp.exp2(level - high[None])
        own = jnp.exp2(own - high)
        first = jnp.exp2(first - high)
        part = part_ref[:, g * HD : (g + 1) * HD].astype(f32).reshape(sources, home_rows, HD)
        mixed = jnp.sum(part * weight, axis=0) + own * value + first * first_value
        mixed = mixed / (jnp.sum(weight, axis=0) + own + first)
        out_ref[:, g * HD : (g + 1) * HD] = jnp.concatenate([mixed] * copies, axis=0).astype(bf16)


def on_device(queries, prefix_k, prefix_v, suffix_k, suffix_v, new_k, new_v, suffix_len, owner_of):
    req_local, tokens, width = queries.shape
    groups = width // HD
    ctx_count = lax.axis_size("ctx")
    head_count = lax.axis_size("head")
    home_rows = req_local * tokens
    all_rows = ctx_count * home_rows
    rows = all_rows * groups
    vmem = pl.BlockSpec(memory_space=pltpu.VMEM)

    sent, home, table = pl.pallas_call(
        functools.partial(spread_kernel, ctx_count),
        in_specs=[vmem] * 5,
        out_specs=[vmem] * 3,
        out_shape=[
            pltpu.VMEM((all_rows, width), bf16),
            pltpu.VMEM((home_rows, width + 2 * HD), f32),
            pltpu.VMEM((2, owner_of.shape[0]), jnp.int32),
        ],
        name="spread",
    )(queries, new_k, new_v, owner_of.reshape(1, -1), suffix_len.reshape(1, -1))
    gathered = lax.all_to_all(sent, "ctx", split_axis=0, concat_axis=0, tiled=True)

    parts, fresh = attend(table, home, gathered, prefix_k, prefix_v, suffix_k, suffix_v)
    arrived = lax.all_to_all(parts, "ctx", split_axis=0, concat_axis=0, tiled=True)

    finished = pl.pallas_call(
        functools.partial(merge_kernel, ctx_count, head_count),
        in_specs=[vmem] * 3,
        out_specs=vmem,
        out_shape=pltpu.VMEM((head_count * home_rows, width), bf16),
        name="merge",
    )(near(arrived), near(fresh), near(home))
    heads = lax.all_to_all(finished, "head", split_axis=0, concat_axis=0, tiled=True)
    heads = heads.reshape(head_count, home_rows, width).transpose(1, 0, 2)
    return heads.reshape(req_local, tokens, head_count * width)


def solution(mesh):
    placed = (
        P("ctx", None, "head"),
        P("ctx", "head"),
        P("ctx", "head"),
        P("ctx", None, "head"),
        P("ctx", None, "head"),
        P("ctx", None, "head"),
        P("ctx", None, "head"),
        P(),
        P(),
    )
    return jax.shard_map(
        on_device, mesh=mesh, in_specs=placed, out_specs=P("ctx", None, None), check_vma=False
    )
```
